256 devices in a mesh: ctx: 64 (over z, x, core), seq: 4 (over y).
Axes of the slice: x: 4, y: 4, z: 8, core: 2. Of those that a mesh axis runs over, the one named last changes fastest.
Arguments:
- x_loader: bfloat16 [32768, 4096], P(('seq', 'ctx')), parts along dimension 0, may hold values from -6 to 6
- b_loader: bfloat16 [32768, 512], P(('seq', 'ctx')), parts along dimension 0, may hold values from -0.75 to 0.75
- c_loader: bfloat16 [32768, 512], P(('seq', 'ctx')), parts along dimension 0, may hold values from -0.75 to 0.75
- dt_loader: bfloat16 [32768, 64], P(('seq', 'ctx')), parts along dimension 0, may hold values from -5 to 5
- local_order: int32 [256, 128], P(('seq', 'ctx')), parts along dimension 0, may hold values from 0 to 127, each once within a row
- resets: int32 [32768], P(('seq', 'ctx')), parts along dimension 0, may hold values 0 or 1
- decay_rate: float32 [64], replicated, may hold values from 0 to 1, as said below
- skip_gain: float32 [64], replicated, may hold values from 0.5 to 1.5
Outputs:
- layer_out: bfloat16 [32768, 4096], P(('seq', 'ctx')), parts along dimension 0
The draws below stay inside these ranges and needn't reach their ends.
There are 4 independent parts, one for each index of `seq`. The reference program is written for one: setup_inputs(seed, part) draws one part's arguments, and reference() takes and returns one part's arrays. A program takes and returns all parts, laid end to end along the dimension named above; an argument that names none is the same for every part. Nothing has to cross between parts.
Inputs may be any that keep to these rules, and one draw needn't show every extreme that they name: Each row of local_order is a permutation of 0 to 127. `decay_rate`: positive rates.
All inputs are finite; a program needn't handle non-finite values. No bound on the sum of `resets` on one device may be relied on, other than what follows from the above.
Results may differ from the reference program's by a relative error of at most 0.0056.
Values may be sent and summed in bfloat16 or wider, within the bound.
No kernel may reach another device: no remote copies, remote signals or barrier semaphores. Data moves between devices by JAX's collectives and lax.ppermute only.
A program may use at most 192 MiB of HBM per device.

```python
import jax
import jax.numpy as jnp
from jax import lax

H = 64
P_SIZE = 64
N = 64
G = 8
SPAN = 128
TOK_DEV = 128
TOKENS = 8192
N_CTX = 64


def draw_decay_rate(key, part):
    key = jax.random.fold_in(key, 11)
    first, second, third = jax.random.split(key, 3)
    slow = jnp.exp(jax.random.uniform(first, (H,), jnp.float32, jnp.log(0.2 / TOKENS), jnp.log(2.0 / TOKENS)))
    fast = jnp.exp(jax.random.uniform(second, (H,), jnp.float32, jnp.log(0.01), jnp.log(0.05)))
    share = 0.5
    picked = jax.random.uniform(third, (H,), jnp.float32) < share
    return jnp.where(picked, slow, fast).astype(jnp.float32)


def set_ends(drawn, rng, least, high):
    longest = drawn.shape.index(max(drawn.shape))
    spots = []
    for shift in (0, 1):
        where = [jax.random.randint(jax.random.fold_in(rng, axis), (), 0, length) for axis, length in enumerate(drawn.shape)]
        where[longest] = (where[longest] + shift) % drawn.shape[longest]
        spots.append(tuple(where))
    return drawn.at[spots[0]].set(least).at[spots[1]].set(high)


def levels(key, shape, cuts, smallest, largest):
    loudness = 1.0
    for dim, parts in cuts:
        steps = jax.random.uniform(jax.random.fold_in(jax.random.fold_in(key, 6), dim), (parts,), jnp.float32, smallest / len(cuts), largest / len(cuts))
        loudness = loudness * jnp.repeat(jnp.exp(steps), shape[dim] // parts).reshape((-1,) + (1,) * (len(shape) - 1 - dim))
    return loudness


def gaussian(key, dims, scale, most, cuts=(), held_as=jnp.bfloat16):
    result = jax.random.normal(key, dims, jnp.float32) * scale
    if len(cuts) > 0:
        result = levels(key, dims, cuts, -0.22, 0.18) * result
    return jnp.clip(result, min=-most, max=most).astype(held_as)


def setup_inputs(seed: int = 0, part: int = 0) -> dict:
    streams_of = jax.random.split(jax.random.key(seed), 9)
    part_keys = jax.random.split(jax.random.fold_in(streams_of[8], part), 9)
    return {
        "x_loader": gaussian(part_keys[0], (TOKENS, H * P_SIZE), 1.0, 6.0, ((0, 64),)),
        "b_loader": gaussian(part_keys[1], (TOKENS, G * N), N ** -0.5, 0.75, ((0, 64),)),
        "c_loader": gaussian(part_keys[2], (TOKENS, G * N), N ** -0.5, 0.75, ((0, 64),)),
        "dt_loader": gaussian(part_keys[3], (TOKENS, H), 1.0, 5.0, ((0, 64),)),
        "local_order": jax.vmap(lambda own: jax.random.permutation(own, TOK_DEV))(jax.random.split(part_keys[4], N_CTX)).reshape((N_CTX, TOK_DEV)).astype(jnp.int32),
        "resets": set_ends((jax.random.randint(part_keys[5], (TOKENS,), 0, 8 * TOK_DEV) < 1).astype(jnp.int32), jax.random.fold_in(part_keys[5], 1), 0, 1),
        "decay_rate": draw_decay_rate(jax.random.fold_in(streams_of[8], 71), part),
        "skip_gain": jnp.clip(1.0 + 0.1 * jax.random.normal(streams_of[7], (H,), jnp.float32), 0.5, 1.5),
    }


def reference(x_loader, b_loader, c_loader, dt_loader, local_order, resets, decay_rate, skip_gain):
    slab_rows = TOK_DEV // N_CTX
    per_group = H // G
    spans = TOKENS // SPAN
    owner = jnp.arange(TOKENS, dtype=jnp.int32) // TOK_DEV
    arrival = local_order.reshape(-1).astype(jnp.int32)
    source = ((arrival // slab_rows) * TOK_DEV + owner * slab_rows + arrival % slab_rows).astype(jnp.int32)
    x_rows = jnp.take(x_loader, source, axis=0).reshape(spans, SPAN, H, P_SIZE)
    b_rows = jnp.take(b_loader, source, axis=0).reshape(spans, SPAN, G, N)
    c_rows = jnp.take(c_loader, source, axis=0).reshape(spans, SPAN, G, N)
    dt_rows = jnp.take(dt_loader, source, axis=0).reshape(spans, SPAN, H)
    reset_rows = resets.reshape(spans, SPAN)
    position = jnp.arange(SPAN, dtype=jnp.int32)
    causal = position[:, None] >= position[None, :]

    def advance(carried, inputs):
        x_here, b_here, c_here, dt_here, reset_here = inputs
        step_size = jax.nn.softplus(dt_here.astype(jnp.float32))
        cumulate = jnp.cumsum(-step_size * decay_rate[None, :], axis=0)
        boundary = jnp.cumsum(reset_here, axis=0)
        keep_mask = causal & (boundary[:, None] == boundary[None, :])
        scores = jnp.einsum("tgn,sgn->gts", c_here.astype(jnp.float32), b_here.astype(jnp.float32))
        cum_heads = cumulate.T.reshape(G, per_group, SPAN)
        gap = cum_heads[:, :, :, None] - cum_heads[:, :, None, :]
        decay = jnp.exp(jnp.where(keep_mask[None, None], gap, -jnp.inf))
        step_heads = step_size.T.reshape(G, per_group, SPAN)
        weights = (scores[:, None] * decay * step_heads[:, :, None, :]).astype(jnp.bfloat16)
        x_heads = x_here.reshape(SPAN, G, per_group, P_SIZE)
        local = jnp.einsum("gjts,sgjp->tgjp", weights.astype(jnp.float32), x_heads.astype(jnp.float32)).reshape(SPAN, H, P_SIZE)
        rounded = lax.optimization_barrier(carried.astype(jnp.bfloat16)).astype(jnp.float32).reshape(G, per_group, P_SIZE, N)
        inter = jnp.einsum("tgn,gjpn->tgjp", c_here.astype(jnp.float32), rounded).reshape(SPAN, H, P_SIZE)
        entry = jnp.exp(cumulate) * (boundary == 0).astype(jnp.float32)[:, None]
        output = local + inter * entry[:, :, None] + skip_gain[None, :, None] * x_here.astype(jnp.float32)
        tail = cumulate[-1:] - cumulate
        weight_in = jnp.exp(tail) * step_size * (boundary[-1:] == boundary).astype(jnp.float32)[:, None]
        x_weighted = (x_here.astype(jnp.float32) * weight_in[:, :, None]).astype(jnp.bfloat16)
        span_state = jnp.einsum("sgjp,sgn->gjpn", x_weighted.astype(jnp.float32).reshape(SPAN, G, per_group, P_SIZE), b_here.astype(jnp.float32)).reshape(H, P_SIZE, N)
        span_decay = jnp.exp(cumulate[-1]) * (boundary[-1] == 0).astype(jnp.float32)
        following = span_decay[:, None, None] * carried + span_state
        return following, output.astype(jnp.bfloat16).reshape(SPAN, H * P_SIZE)

    start = jnp.zeros((H, P_SIZE, N), jnp.float32)
    finished, outputs = lax.scan(advance, start, (x_rows, b_rows, c_rows, dt_rows, reset_rows))
    return outputs.reshape(TOKENS, H * P_SIZE)
```

```python
import jax
import jax.numpy as jnp
from jax import lax
from jax.experimental import pallas as pl
from jax.experimental.pallas import tpu as pltpu
from jax.sharding import Mesh, PartitionSpec as P

F32 = jnp.float32
BF16 = jnp.bfloat16
I32 = jnp.int32
T = 128
NZ = 8
NW = 8
HG = 8
HP = 64
N = 64
GW = HG * HP
MSG = 88
VMEM = 48 * 1024 * 1024


def iota(shape, dim):
    return lax.broadcasted_iota(I32, shape, dim)


def dot(a, b):
    return jnp.dot(a, b, preferred_element_type=F32)


def params():
    return pltpu.CompilerParams(vmem_limit_bytes=VMEM)


def pack_kernel(x_ref, b_ref, c_ref, dt_ref, order_ref, reset_ref, out_ref):
    head, lane = iota((64, 1024), 0), iota((64, 1024), 1)
    spread = (lane % 128 < 64) & (head == (lane // 128) * 8 + lane % 8)
    wide = dot(dt_ref[...], spread.astype(BF16))
    row, lane = iota((T, 1024), 0), iota((T, 1024), 1)
    wide = jnp.where((row // 2) % 8 == (lane % 128) // 8, wide, 0.0).astype(BF16)
    to, row = iota((64, T), 0), iota((64, T), 1)
    pick = (row // 16 == to // 8) & (row % 2 == to % 8)
    steps = dot(pick.astype(BF16), wide)
    upto = (iota((T, T), 0) <= iota((T, T), 1)).astype(BF16)
    resets = jnp.broadcast_to(reset_ref[...].astype(F32), (8, T)).astype(BF16)
    count = dot(resets, upto)
    order = jnp.broadcast_to(order_ref[...].astype(F32), (8, T))
    own = iota((8, T), 1) % 8 == iota((8, T), 0)
    place = iota((T, T), 1) - iota((T, T), 0) // 8
    extra = dot(jnp.where(own, order, 0.0).astype(BF16), (place == 64).astype(BF16))
    extra += dot(jnp.where(own, count, 0.0).astype(BF16), (place == 80).astype(BF16))
    for z in range(NZ):
        rows = pl.ds(16 * z, 16)
        for g in range(NW):
            m = z * NW + g
            for j in range(4):
                out_ref[m, pl.ds(16 * j, 16), :] = x_ref[rows, pl.ds(GW * g + 128 * j, 128)]
            b = b_ref[rows, pl.ds(128 * (g // 2), 128)]
            c = c_ref[rows, pl.ds(128 * (g // 2), 128)]
            lo = N * (g % 2)
            out_ref[m, pl.ds(64, 16), :] = jnp.concatenate(
                [b[:, lo : lo + N], c[:, lo : lo + N]], axis=1
            )
            tail = steps[8 * z : 8 * z + 8, 128 * g : 128 * g + 128] + extra
            out_ref[m, pl.ds(80, 8), :] = tail.astype(BF16)


def expander():
    return (iota((T, GW), 0) % 8 == iota((T, GW), 1) // HP).astype(BF16)


def two_parts(v):
    high = v.astype(BF16).astype(F32)
    low = v - high
    return jnp.where(iota(v.shape, 1) < 64, high, pltpu.roll(low, 64, 1))


def expand(parts, i, e):
    mine = (iota(parts.shape, 1) % 64) // 8 == i
    return dot(jnp.where(mine, parts, 0.0).astype(BF16), e)


def state_kernel(
    arrived_ref, rate_ref, x_ref, bc_ref, cum_ref, key_ref, entry_ref, carry_ref, count_ref, hin_ref, msg_ref, perm_ref
):
    z = lax.axis_index("z")
    tails = jnp.concatenate(
        [arrived_ref[z * 8 + i, pl.ds(80, 8), :].astype(F32) for i in range(8)], axis=0
    ).astype(BF16)
    row, col = iota((1024, 64), 0), iota((1024, 64), 1)
    sel = (col == (row // T) * 8 + row % 8).astype(BF16)
    spread = dot(sel, tails)
    lane = iota((1024, T), 1)
    block = (iota((1024, T), 0) % T) // 8
    spread = jnp.where((lane == 64 + block) | (lane == 80 + block), spread, 0.0).astype(BF16)
    src, dst = iota((T, 256), 0), iota((T, 256), 1)
    gather = ((src >= 64) & (src < 80) & (dst < T)) | ((src >= 80) & (src < 96) & (dst >= T))
    both = dot(spread, gather.astype(BF16))
    order = both[:, :T].astype(I32)
    count = both[:, T:]
    count_ref[...] = count
    span = iota((1024, T), 0) // T
    target = (order // 2) * 16 + 2 * span + order % 2
    for m in range(8):
        perm_ref[:, pl.ds(128 * m, 128)] = jnp.where(lane + 128 * m == target, 1.0, 0.0).astype(BF16)
    rows = jnp.concatenate(
        [arrived_ref[:, pl.ds(16 * j, 16), :].reshape(1024, 128) for j in range(5)], axis=1
    )
    rows = dot(perm_ref[...], rows).astype(BF16)
    x_ref[...] = rows[:, :GW]
    bc_ref[...] = rows[:, GW:]
    steps_in = arrived_ref[:, pl.ds(80, 8), :].astype(F32).reshape(512, 128).astype(BF16)
    target = (order // 2) * 8 + order % 2
    small = jnp.concatenate(
        [jnp.where(lane + 128 * m == target, 1.0, 0.0).astype(BF16) for m in range(4)], axis=1
    )
    raw_all = dot(small, steps_in)
    lane = iota((T, T), 1)
    raw = jnp.zeros((T, T), F32)
    cnt = jnp.zeros((T, T), F32)
    for i in range(8):
        raw = jnp.where(lane // 8 == i, raw_all[T * i : T * i + T], raw)
        cnt = jnp.where(lane // 8 == i, count[T * i : T * i + T], cnt)
    step = jnp.maximum(raw, 0.0) + jnp.log1p(jnp.exp(-jnp.abs(raw)))
    logd = -step * rate_ref[...]
    lower = (iota((T, T), 0) >= iota((T, T), 1)).astype(F32)
    cum = jnp.dot(lower, logd, preferred_element_type=F32, precision=lax.Precision.HIGHEST)
    cum_ref[...] = cum
    key_ref[...] = (cum - jnp.log(step)).T
    last = cum[T - 1 : T]
    last_cnt = cnt[T - 1 : T]
    entry = jnp.where(cnt == 0.0, jnp.exp(cum), 0.0)
    entry_ref[...] = entry
    decay = jnp.where(last_cnt == 0.0, jnp.exp(last), 0.0)
    decay = jnp.broadcast_to(decay, (8, T))
    lane8 = iota((8, T), 1)
    before = jnp.where(lane8 < 8, 1.0, pltpu.roll(decay, 8, 1))
    for shift in (8, 16, 32):
        before = before * jnp.where(lane8 < shift, 1.0, pltpu.roll(before, shift, 1))
    carry_ref[...] = entry * before[:1]
    coef = jnp.where(cnt == last_cnt, jnp.exp(last - cum) * step, 0.0)
    e = expander()
    coef = two_parts(coef)
    mine = (lane8 % 64) // 8 == iota((8, T), 0)
    decay = dot(jnp.where(mine, two_parts(decay), 0.0).astype(BF16), e)
    h = jnp.zeros((N, GW), F32)
    total = jnp.ones((1, GW), F32)
    for i in range(8):
        here = pl.ds(T * i, T)
        hin_ref[i] = h.astype(BF16)
        xw = (x_ref[here, :].astype(F32) * expand(coef, i, e)).astype(BF16)
        b = bc_ref[here, :].astype(F32).T[:N].astype(BF16)
        h = decay[i : i + 1] * h + dot(b, xw)
        total = total * decay[i : i + 1]
    high = total.astype(BF16).astype(F32)
    mid = (total - high).astype(BF16).astype(F32)
    low = total - high - mid
    row = iota((16, GW), 0)
    parts = jnp.where(row == 0, high, jnp.where(row == 1, mid, jnp.where(row == 2, low, 0.0)))
    for m in range(8):
        lanes = slice(128 * (m // 2), 128 * (m // 2) + 128)
        msg_ref[m, pl.ds(0, 32), :] = h[32 * (m % 2) : 32 * (m % 2) + 32, lanes].astype(BF16)
        msg_ref[m, pl.ds(32, 16), :] = parts[:, lanes].astype(BF16)


def local_kernel(x_ref, bc_ref, cum_ref, key_ref, entry_ref, count_ref, hin_ref, skip_ref, out_ref):
    e = expander()
    entry = two_parts(entry_ref[...])
    causal = iota((T, T), 0) >= iota((T, T), 1)
    left = iota((T, T), 1) < HP
    for i in range(8):
        here = pl.ds(T * i, T)
        count = count_ref[here, :]
        keep = causal & (count == count.T)
        bc = bc_ref[here, :]
        b = bc.astype(F32).T[:N].astype(BF16)
        scores = dot(bc[:, N:], b)
        carried = dot(bc[:, N:], hin_ref[i]) * expand(entry, i, e)
        for pair in range(4):
            weights = []
            for h in (2 * pair, 2 * pair + 1):
                c = 8 * i + h
                gap = cum_ref[:, c : c + 1] - key_ref[c : c + 1, :]
                weights.append((jnp.exp(jnp.where(keep, gap, -jnp.inf)) * scores).astype(BF16))
            lanes = pl.ds(128 * pair, 128)
            x = x_ref[here, lanes]
            zero = jnp.zeros_like(x)
            both = jnp.concatenate([jnp.where(left, x, zero), jnp.where(left, zero, x)], axis=0)
            local = dot(jnp.concatenate(weights, axis=1), both)
            out_ref[here, lanes] = (
                local + carried[:, 128 * pair : 128 * pair + 128] + skip_ref[:, lanes] * x.astype(F32)
            )


def scan_kernel(in_ref, out_ref):
    h = jnp.zeros((32, 128), F32)
    for z in range(NZ):
        out_ref[z] = h.astype(BF16)
        parts = in_ref[z, pl.ds(32, 16), :].astype(F32)
        decay = parts[0:1] + parts[1:2] + parts[2:3]
        h = decay * h + in_ref[z, pl.ds(0, 32), :].astype(F32)


def final_kernel(partial_ref, bc_ref, carry_ref, h_ref, out_ref):
    e = expander()
    carry = two_parts(carry_ref[...])
    state = jnp.concatenate(
        [jnp.concatenate([h_ref[2 * p], h_ref[2 * p + 1]], axis=0) for p in range(4)], axis=1
    )
    for i in range(8):
        here = pl.ds(T * i, T)
        inter = dot(bc_ref[here, :][:, N:], state) * expand(carry, i, e)
        out_ref[i] = (partial_ref[here, :] + inter).astype(BF16)


def join_kernel(in_ref, out_ref):
    for g in range(NW):
        out_ref[:, pl.ds(GW * g, GW)] = in_ref[g]


def per_device(x, b, c, dt, order, resets, rate, skip):
    w = lax.axis_index("w")
    sds = jax.ShapeDtypeStruct
    packed = pl.pallas_call(
        pack_kernel, out_shape=sds((NZ * NW, MSG, 128), BF16), compiler_params=params(), name="pack"
    )(x, b, c, dt, order, resets.reshape(1, T))
    arrived = lax.all_to_all(packed, ("z", "w"), split_axis=0, concat_axis=0, tiled=True)
    mine = lax.dynamic_slice_in_dim(rate, w * HG, HG)
    rate_row = jnp.concatenate([jnp.tile(mine, 8), jnp.zeros((64,), F32)]).reshape(1, T)
    skip_row = jnp.repeat(lax.dynamic_slice_in_dim(skip, w * HG, HG), HP).reshape(1, GW)
    xs, bc, cum, key, entry, carry, count, hin, msg = pl.pallas_call(
        state_kernel,
        out_shape=(
            sds((NZ * T, GW), BF16),
            sds((NZ * T, 128), BF16),
            sds((T, T), F32),
            sds((T, T), F32),
            sds((T, T), F32),
            sds((T, T), F32),
            sds((NZ * T, T), F32),
            sds((8, N, GW), BF16),
            sds((NZ, 48, 128), BF16),
        ),
        scratch_shapes=[pltpu.VMEM((1024, 1024), BF16)],
        compiler_params=params(),
        name="state",
    )(arrived, rate_row)
    totals = lax.all_to_all(msg, "z", split_axis=0, concat_axis=0, tiled=True)
    partial = pl.pallas_call(
        local_kernel,
        out_shape=sds((NZ * T, GW), F32),
        compiler_params=params(),
        cost_estimate=pl.CostEstimate(flops=600_000_000, bytes_accessed=6_000_000, transcendentals=1_100_000),
        name="local",
    )(xs, bc, cum, key, entry, count, hin, skip_row)
    entering = pl.pallas_call(
        scan_kernel, out_shape=sds((NZ, 32, 128), BF16), compiler_params=params(), name="planes"
    )(totals)
    states = lax.all_to_all(entering, "z", split_axis=0, concat_axis=0, tiled=True)
    out = pl.pallas_call(
        final_kernel,
        out_shape=sds((8, T, GW), BF16),
        compiler_params=params(),
        name="final",
    )(partial, bc, carry, states)
    owned = lax.all_to_all(out, "w", split_axis=0, concat_axis=0, tiled=True)
    return pl.pallas_call(
        join_kernel, out_shape=sds((T, NW * GW), BF16), compiler_params=params(), name="join"
    )(owned)


def solution(mesh):
    fine = Mesh(mesh.devices.reshape(NZ, NW, mesh.shape["seq"]), ("z", "w", "seq"))
    rows = ("seq", "z", "w")
    in_specs = (P(rows, None),) * 5 + (P(rows), P(), P())
    return jax.shard_map(
        per_device, mesh=fine, in_specs=in_specs, out_specs=P(rows, None), check_vma=False
    )
```

```python
import jax
import jax.numpy as jnp
from jax import lax
from jax.experimental import pallas as pl
from jax.experimental.pallas import tpu as pltpu
from jax.sharding import Mesh, PartitionSpec as P

F32 = jnp.float32
BF16 = jnp.bfloat16
I32 = jnp.int32
T = 128
NP = 32
HG = 8
HP = 64
N = 64
GW = HG * HP
HH = 32
HW = HH * HP
MSG = 88


def iota(shape, dim):
    return lax.broadcasted_iota(I32, shape, dim)


def dot(a, b):
    return jnp.dot(a, b, preferred_element_type=F32)


def dot_nt(a, b):
    return lax.dot_general(a, b, (((1,), (1,)), ((), ())), preferred_element_type=F32)


def params(mib):
    return pltpu.CompilerParams(vmem_limit_bytes=mib * 1024 * 1024)


def pack_kernel(x_hbm, b_hbm, c_hbm, dt_hbm, order_hbm, reset_hbm, out_ref, x_ref, b_ref, c_ref, dt_ref, order_ref, reset_ref, sems):
    pairs = (
        (order_hbm, order_ref), (reset_hbm, reset_ref), (dt_hbm, dt_ref),
        (b_hbm, b_ref), (c_hbm, c_ref), (x_hbm, x_ref),
    )
    copies = [pltpu.make_async_copy(s, d, sems.at[n]) for n, (s, d) in enumerate(pairs)]
    for copy in copies:
        copy.start()
    row, col = iota((256, 256), 0), iota((256, 256), 1)
    pick = (col // 64 == (row % 16) // 4) & (col % 64 == (row // 16) * 4 + row % 4)
    pick = pick.astype(BF16)
    lane, head = iota((256, 64), 0), iota((256, 64), 1)
    spread = (lane % T < 64) & (head == (lane // T) * HH + lane % HH)
    to, row = iota((256, T), 0), iota((256, T), 1)
    own_row = ((row // 4 == to // 8) & (row % 2 == to % 8)).astype(BF16)
    own_span = (row // 2) % 2 == (to % T) // HH
    upto = (iota((T, T), 0) <= iota((T, T), 1)).astype(BF16)
    own = iota((8, T), 1) % 8 == iota((8, T), 0)
    place = iota((T, T), 1) - iota((T, T), 0) // 8
    for copy in copies[:3]:
        copy.wait()
    wide = jnp.where(own_span, dot(spread.astype(BF16), dt_ref[...]), 0.0).astype(BF16)
    steps = dot_nt(own_row, wide)
    resets = jnp.broadcast_to(reset_ref[...].astype(F32), (8, T)).astype(BF16)
    count = dot(resets, upto)
    order = jnp.broadcast_to(order_ref[...].astype(F32), (8, T))
    extra = dot(jnp.where(own, order, 0.0).astype(BF16), (place == 64).astype(BF16))
    extra += dot(jnp.where(own, count, 0.0).astype(BF16), (place == 80).astype(BF16))
    for p in range(NP):
        for c in range(2):
            tail = steps[8 * p : 8 * p + 8, T * c : T * c + T] + extra
            out_ref[2 * p + c, pl.ds(80, 8), :] = tail.astype(BF16)
    for copy in copies[3:]:
        copy.wait()
    for part in range(2):
        rows = pl.ds(64 * part, 64)
        tiles = []
        for c in range(2):
            for q in range(4):
                tiles.append([x_ref[rows, pl.ds(HW * c + 512 * q + T * j, T)] for j in range(4)])
            tiles.append(
                [b_ref[rows, pl.ds(256 * c, T)], b_ref[rows, pl.ds(256 * c + T, T)],
                 c_ref[rows, pl.ds(256 * c, T)], c_ref[rows, pl.ds(256 * c + T, T)]]
            )
        right = jnp.concatenate([jnp.concatenate(t, axis=0) for t in tiles], axis=1)
        got = dot(pick, right).astype(BF16)
        for p in range(16):
            for c in range(2):
                for q in range(5):
                    lanes = slice(T * (5 * c + q), T * (5 * c + q) + T)
                    out_ref[2 * (16 * part + p) + c, pl.ds(16 * q, 16), :] = got[16 * p : 16 * p + 16, lanes]


def expander():
    return (iota((T, HW), 0) % HH == iota((T, HW), 1) // HP).astype(BF16)


def two_parts(v):
    high = v.astype(BF16).astype(F32)
    low = v - high
    return jnp.where(iota(v.shape, 1) < 64, high, pltpu.roll(low, 64, 1))


def of_span(parts, i):
    return jnp.where((iota(parts.shape, 1) % 64) // HH == i, parts, 0.0).astype(BF16)


def state_kernel(
    arrived_ref, rate_ref, x_ref, bc_ref, cum_ref, key_ref, entry_ref, carry_ref, count_ref, hin_ref, msg_ref, perm_ref
):
    chip = lax.axis_index("p")
    tails = jnp.concatenate(
        [arrived_ref[chip * 2 + i, pl.ds(80, 8), :].astype(F32) for i in range(2)], axis=0
    ).astype(BF16)
    row, col = iota((256, 16), 0), iota((256, 16), 1)
    sel = (col == (row // T) * 8 + row % 8).astype(BF16)
    spread = dot(sel, tails)
    lane = iota((256, T), 1)
    block = (iota((256, T), 0) % T) // 8
    spread = jnp.where((lane == 64 + block) | (lane == 80 + block), spread, 0.0).astype(BF16)
    src, dst = iota((T, 256), 0), iota((T, 256), 1)
    gather = ((src >= 64) & (src < 80) & (dst < T)) | ((src >= 80) & (src < 96) & (dst >= T))
    both = dot(spread, gather.astype(BF16))
    order = both[:, :T].astype(I32)
    count = both[:, T:]
    count_ref[...] = count
    target = (order // 2) * 16 + 2 * (iota((256, T), 0) // T) + order % 2
    for j in range(4):
        for m in range(8):
            hit = lane + (T * m - 4 * j) == target
            perm_ref[pl.ds(256 * j, 256), pl.ds(T * m, T)] = jnp.where(hit, 1.0, 0.0).astype(BF16)
    rows = jnp.concatenate(
        [arrived_ref[:, pl.ds(16 * q, 16), :].reshape(1024, T) for q in range(5)], axis=1
    )
    rows = dot(perm_ref[...], rows).astype(BF16)
    for j in range(4):
        for q in range(4):
            x_ref[:, pl.ds(T * (4 * q + j), T)] = rows[256 * j : 256 * j + 256, T * q : T * q + T]
        bc_ref[:, pl.ds(T * j, T)] = rows[256 * j : 256 * j + 256, T * 4 :]
    steps_in = arrived_ref[:, pl.ds(80, 8), :].astype(F32).reshape(512, T).astype(BF16)
    target = (order // 2) * 8 + order % 2
    small = jnp.concatenate(
        [jnp.where(lane + T * m == target, 1.0, 0.0).astype(BF16) for m in range(4)], axis=1
    )
    raw = dot(small, steps_in)
    first = iota((T, T), 1) < HH
    raw = jnp.where(first, raw[:T], raw[T:])
    cnt = jnp.where(first, count[:T], count[T:])
    step = jnp.maximum(raw, 0.0) + jnp.log1p(jnp.exp(-jnp.abs(raw)))
    logd = -step * rate_ref[...]
    lower = (iota((T, T), 0) >= iota((T, T), 1)).astype(F32)
    cum = jnp.dot(lower, logd, preferred_element_type=F32, precision=lax.Precision.HIGHEST)
    cum_ref[...] = cum
    key_ref[...] = (cum - jnp.log(step)).T
    last = cum[T - 1 : T]
    last_cnt = cnt[T - 1 : T]
    entry = jnp.where(cnt == 0.0, jnp.exp(cum), 0.0)
    entry_ref[...] = entry
    decay = jnp.where(last_cnt == 0.0, jnp.exp(last), 0.0)
    decay = jnp.broadcast_to(decay, (8, T))
    before = jnp.where(iota((8, T), 1) < HH, 1.0, pltpu.roll(decay, HH, 1))
    carry_ref[...] = entry * before[:1]
    coef = two_parts(jnp.where(cnt == last_cnt, jnp.exp(last - cum) * step, 0.0))
    e = expander()
    decay = two_parts(decay)
    decay = [dot(of_span(decay, i), e)[:1] for i in range(2)]
    total = decay[0] * decay[1]
    weighted = []
    for i in range(2):
        here = pl.ds(T * i, T)
        weighted.append((x_ref[here, :].astype(F32) * dot(of_span(coef, i), e)).astype(BF16))
    high = total.astype(BF16).astype(F32)
    mid = (total - high).astype(BF16).astype(F32)
    low = total - high - mid
    row = iota((8, HW), 0)
    parts = jnp.where(row == 0, high, jnp.where(row == 1, mid, jnp.where(row == 2, low, 0.0))).astype(BF16)
    for tile in range(2):
        b = [bc_ref[pl.ds(T * i, T), pl.ds(T * tile, T)].astype(F32).T.astype(BF16) for i in range(2)]
        for half in range(2):
            g = 2 * tile + half
            lanes = slice(GW * g, GW * g + GW)
            states = [dot(b[i][N * half : N * half + N], weighted[i][:, lanes]) for i in range(2)]
            hin_ref[:, lanes] = states[0].astype(BF16)
            h = (decay[1][:, lanes] * states[0] + states[1]).astype(BF16)
            for pair in range(4):
                for k in range(2):
                    m = (4 * g + pair) * 2 + k
                    msg_ref[m, pl.ds(0, 32), :] = h[32 * k : 32 * k + 32, T * pair : T * pair + T]
    for m in range(NP):
        msg_ref[m, pl.ds(32, 8), :] = parts[:, T * (m // 2) : T * (m // 2) + T]


def local_kernel(x_ref, bc_ref, cum_ref, key_ref, entry_ref, count_ref, hin_ref, skip_ref, out_ref):
    e = expander()
    entry = dot(of_span(two_parts(entry_ref[...]), 1), e)
    causal = iota((T, T), 0) >= iota((T, T), 1)
    left = iota((T, T), 1) < HP
    for i in range(2):
        here = pl.ds(T * i, T)
        count = count_ref[here, :]
        keep = causal & (count == count.T)
        for g in range(4):
            tile, half = g // 2, g % 2
            b = bc_ref[here, pl.ds(T * tile, T)][:, N * half : N * half + N]
            c = bc_ref[here, pl.ds(2 * T + T * tile, T)][:, N * half : N * half + N]
            scores = dot_nt(c, b)
            if i == 1:
                lanes = pl.ds(GW * g, GW)
                carried = dot(c, hin_ref[:, lanes]) * entry[:, GW * g : GW * g + GW]
            for pair in range(4):
                weights = []
                for h in (2 * pair, 2 * pair + 1):
                    col = HH * i + HG * g + h
                    gap = cum_ref[:, col : col + 1] - key_ref[col : col + 1, :]
                    weights.append((jnp.exp(jnp.where(keep, gap, -jnp.inf)) * scores).astype(BF16))
                lanes = pl.ds(GW * g + T * pair, T)
                x = x_ref[here, lanes]
                zero = jnp.zeros_like(x)
                both = jnp.concatenate([jnp.where(left, x, zero), jnp.where(left, zero, x)], axis=0)
                out = dot(jnp.concatenate(weights, axis=1), both) + skip_ref[:, lanes] * x.astype(F32)
                if i == 1:
                    out += carried[:, T * pair : T * pair + T]
                out_ref[here, lanes] = out


def scan_kernel(in_ref, out_ref):
    h = jnp.zeros((32, T), F32)
    for p in range(NP):
        out_ref[p] = h.astype(BF16)
        parts = in_ref[p, pl.ds(32, 8), :].astype(F32)
        decay = parts[0:1] + parts[1:2] + parts[2:3]
        h = decay * h + in_ref[p, pl.ds(0, 32), :].astype(F32)


def final_kernel(partial_ref, bc_ref, carry_ref, h_ref, mine_ref, other_ref):
    core = lax.axis_index("c")
    e = expander()
    carry = two_parts(carry_ref[...])
    for ref, i in ((other_ref, 1 - core), (mine_ref, core)):
        here = pl.ds(pl.multiple_of(T * i, T), T)
        scale = dot(of_span(carry, i), e)
        for g in range(4):
            c = bc_ref[here, pl.ds(2 * T + T * (g // 2), T)][:, N * (g % 2) : N * (g % 2) + N]
            state = jnp.concatenate(
                [jnp.concatenate([h_ref[8 * g + 2 * p], h_ref[8 * g + 2 * p + 1]], axis=0) for p in range(4)], axis=1
            )
            lanes = slice(GW * g, GW * g + GW)
            inter = dot(c, state) * scale[:, lanes]
            ref[:, lanes] = (partial_ref[here, lanes] + inter).astype(BF16)


def join_kernel(mine_ref, other_ref, out_ref):
    core = lax.axis_index("c")
    for k in range(2):

        @pl.when(core == k)
        def _():
            out_ref[:, pl.ds(HW * k, HW)] = mine_ref[...]
            out_ref[:, pl.ds(HW * (1 - k), HW)] = other_ref[...]


def per_device(x, b, c, dt, order, resets, rate, skip):
    core = lax.axis_index("c")
    sds = jax.ShapeDtypeStruct
    packed = pl.pallas_call(
        pack_kernel,
        out_shape=sds((2 * NP, MSG, T), BF16),
        in_specs=[pl.BlockSpec(memory_space=pltpu.HBM)] * 6,
        scratch_shapes=[
            pltpu.VMEM(x.shape, BF16),
            pltpu.VMEM(b.shape, BF16),
            pltpu.VMEM(c.shape, BF16),
            pltpu.VMEM(dt.shape[::-1], BF16),
            pltpu.VMEM((1, T), I32),
            pltpu.VMEM((1, T), I32),
            pltpu.SemaphoreType.DMA((6,)),
        ],
        compiler_params=params(20),
        name="pack",
    )(x, b, c, dt.T, order, resets.reshape(1, T))
    arrived = lax.all_to_all(packed, ("p", "c"), split_axis=0, concat_axis=0, tiled=True)
    mine = lax.dynamic_slice_in_dim(rate, core * HH, HH)
    rate_row = jnp.concatenate([mine, mine, jnp.zeros((64,), F32)]).reshape(1, T)
    skip_row = jnp.repeat(lax.dynamic_slice_in_dim(skip, core * HH, HH), HP).reshape(1, HW)
    xs, bc, cum, key, entry, carry, count, hin, msg = pl.pallas_call(
        state_kernel,
        out_shape=(
            sds((2 * T, HW), BF16),
            sds((2 * T, 4 * T), BF16),
            sds((T, T), F32),
            sds((T, T), F32),
            sds((T, T), F32),
            sds((T, T), F32),
            sds((2 * T, T), F32),
            sds((N, HW), BF16),
            sds((NP, 40, T), BF16),
        ),
        scratch_shapes=[pltpu.VMEM((1024, 1024), BF16)],
        compiler_params=params(24),
        name="state",
    )(arrived, rate_row)
    totals = lax.all_to_all(msg, "p", split_axis=0, concat_axis=0, tiled=True)
    partial = pl.pallas_call(
        local_kernel,
        out_shape=sds((2 * T, HW), F32),
        compiler_params=params(20),
        cost_estimate=pl.CostEstimate(flops=2_000_000_000, bytes_accessed=6_000_000, transcendentals=1_100_000),
        name="local",
    )(xs, bc, cum, key, entry, count, hin, skip_row)
    entering = pl.pallas_call(
        scan_kernel, out_shape=sds((NP, 32, T), BF16), compiler_params=params(16), name="chips"
    )(totals)
    states = lax.all_to_all(entering, "p", split_axis=0, concat_axis=0, tiled=True)
    own, other = pl.pallas_call(
        final_kernel,
        out_shape=(sds((T, HW), BF16), sds((T, HW), BF16)),
        compiler_params=params(20),
        name="final",
    )(partial, bc, carry, states)
    other = lax.ppermute(other, "c", [(0, 1), (1, 0)])
    return pl.pallas_call(
        join_kernel, out_shape=sds((T, 2 * HW), BF16), compiler_params=params(16), name="join"
    )(own, other)


def solution(mesh):
    fine = Mesh(mesh.devices.reshape(NP, 2, mesh.shape["seq"]), ("p", "c", "seq"))
    rows = ("seq", "p", "c")
    in_specs = (P(rows, None),) * 5 + (P(rows), P(), P())
    return jax.shard_map(
        per_device, mesh=fine, in_specs=in_specs, out_specs=P(rows, None), check_vma=False
    )
```

```python
import jax
import jax.numpy as jnp
from jax import lax
from jax.experimental import pallas as pl
from jax.experimental.pallas import tpu as pltpu
from jax.sharding import Mesh, PartitionSpec as P

F32 = jnp.float32
BF16 = jnp.bfloat16
I32 = jnp.int32
T = 128
NX, NZ = 4, 8
NP = NX * NZ
HG = 8
HP = 64
N = 64
GW = HG * HP
HH = 32
HW = HH * HP
MSG = 88
PARTS = 4


def iota(shape, dim):
    return lax.broadcasted_iota(I32, shape, dim)


def dot(a, b):
    return jnp.dot(a, b, preferred_element_type=F32)


def dot_nt(a, b):
    return lax.dot_general(a, b, (((1,), (1,)), ((), ())), preferred_element_type=F32)


def params(mib):
    return pltpu.CompilerParams(vmem_limit_bytes=mib * 1024 * 1024)


def softplus(v):
    return jnp.maximum(v, 0.0) + jnp.log1p(jnp.exp(-jnp.abs(v)))


def pack_kernel(
    x_hbm, b_hbm, c_hbm, dt_hbm, order_hbm, reset_hbm, out_hbm,
    x_ref, b_ref, c_ref, dt_ref, order_ref, reset_ref, out_ref, sems, out_sems,
):
    pairs = [(order_hbm, order_ref), (reset_hbm, reset_ref), (dt_hbm, dt_ref)]
    span = T // PARTS
    for part in range(PARTS):
        rows = pl.ds(span * part, span)
        pairs += [(src.at[rows], dst.at[rows]) for src, dst in ((b_hbm, b_ref), (c_hbm, c_ref), (x_hbm, x_ref))]
    copies = [pltpu.make_async_copy(s, d, sems.at[n]) for n, (s, d) in enumerate(pairs)]
    for copy in copies:
        copy.start()
    row, col = iota((4 * span, 4 * span), 0), iota((4 * span, 4 * span), 1)
    pick = (col // span == (row % 16) // 4) & (col % span == (row // 16) * 4 + row % 4)
    pick = pick.astype(BF16)
    lane, head = iota((256, 64), 0), iota((256, 64), 1)
    spread = (lane % T < 64) & (head == (lane // T) * HH + lane % HH)
    to, row = iota((256, T), 0), iota((256, T), 1)
    own_row = ((row // 4 == to // 8) & (row % 2 == to % 8)).astype(BF16)
    own_span = (row // 2) % 2 == (to % T) // HH
    upto = (iota((T, T), 0) <= iota((T, T), 1)).astype(BF16)
    own = iota((8, T), 1) % 8 == iota((8, T), 0)
    place = iota((T, T), 1) - iota((T, T), 0) // 8
    to_part, part = iota((256, 192), 0), iota((256, 192), 1)
    rr = to_part % 8 - 2
    chosen = (rr >= 0) & (part // 64 == rr // 2) & (part % 64 == 2 * (to_part // 8) + rr % 2)
    chosen = chosen.astype(BF16)
    of_chip = (iota((T, T), 0) // 4 == iota((T, T), 1)).astype(F32)
    for copy in copies[:6]:
        copy.wait()
    sums = jnp.dot(
        softplus(dt_ref[...].astype(F32)), of_chip, preferred_element_type=F32, precision=lax.Precision.HIGHEST
    )
    high = sums.astype(BF16)
    mid = (sums - high.astype(F32)).astype(BF16)
    low = (sums - high.astype(F32) - mid.astype(F32)).astype(BF16)
    sums = dot(chosen, jnp.concatenate([high, mid, low], axis=0))
    wide = jnp.where(own_span, dot(spread.astype(BF16), dt_ref[...]), 0.0).astype(BF16)
    steps = dot_nt(own_row, wide)
    resets = jnp.broadcast_to(reset_ref[...].astype(F32), (8, T)).astype(BF16)
    count = dot(resets, upto)
    order = jnp.broadcast_to(order_ref[...].astype(F32), (8, T))
    extra = dot(jnp.where(own, order, 0.0).astype(BF16), (place == 64).astype(BF16))
    extra += dot(jnp.where(own, count, 0.0).astype(BF16), (place == 80).astype(BF16))
    sent = []
    for part in range(PARTS):
        if part > 0:
            for copy in copies[3 + 3 * part : 6 + 3 * part]:
                copy.wait()
        rows = pl.ds(span * part, span)
        tiles = []
        for c in range(2):
            for q in range(4):
                tiles.append([x_ref[rows, pl.ds(HW * c + 512 * q + T * j, T)] for j in range(4)])
            tiles.append(
                [b_ref[rows, pl.ds(256 * c, T)], b_ref[rows, pl.ds(256 * c + T, T)],
                 c_ref[rows, pl.ds(256 * c, T)], c_ref[rows, pl.ds(256 * c + T, T)]]
            )
        right = jnp.concatenate([jnp.concatenate(t, axis=0) for t in tiles], axis=1)
        got = dot(pick, right).astype(BF16)
        for p in range(NP // PARTS):
            z, x = NZ // PARTS * part + p // NX, p % NX
            at = 8 * (NP // PARTS * part + p)
            for c in range(2):
                to = 2 * x + c
                for q in range(5):
                    lanes = slice(T * (5 * c + q), T * (5 * c + q) + T)
                    out_ref[to, z, pl.ds(16 * q, 16), :] = got[16 * p : 16 * p + 16, lanes]
                m = 8 * (16 * c + (NZ * x + z) // 2)
                tail = steps[at : at + 8, T * c : T * c + T] + sums[m : m + 8] + extra
                out_ref[to, z, pl.ds(80, 8), :] = tail.astype(BF16)
        here = pl.ds(NZ // PARTS * part, NZ // PARTS)
        sent.append(pltpu.make_async_copy(out_ref.at[:, here], out_hbm.at[:, here], out_sems.at[part]))
        sent[-1].start()
    for copy in sent:
        copy.wait()


def expander():
    return (iota((T, HW), 0) % HH == iota((T, HW), 1) // HP).astype(BF16)


def two_parts(v):
    high = v.astype(BF16).astype(F32)
    low = v - high
    return jnp.where(iota(v.shape, 1) < 64, high, pltpu.roll(low, 64, 1))


def of_span(parts, i):
    return jnp.where((iota(parts.shape, 1) % 64) // HH == i, parts, 0.0).astype(BF16)


def state_kernel(
    arrived_hbm, rate_ref, x_ref, bc_ref, cum_ref, key_ref, entry_ref, carry_ref, count_ref, hin_ref, msg_ref,
    sums_ref, resets_ref, arrived_ref, sems,
):
    copies = []
    for n, rows in enumerate((pl.ds(80, 8), pl.ds(0, 80))):
        copies.append(pltpu.make_async_copy(arrived_hbm.at[:, rows], arrived_ref.at[:, rows], sems.at[n]))
        copies[-1].start()
    plane, column = lax.axis_index("z"), lax.axis_index("x")
    copies[0].wait()
    tails = jnp.concatenate(
        [arrived_ref[(column * 2 + i) * NZ + plane, pl.ds(80, 8), :].astype(F32) for i in range(2)], axis=0
    ).astype(BF16)
    row, col = iota((256, 16), 0), iota((256, 16), 1)
    sel = (col == (row // T) * 8 + row % 8).astype(BF16)
    spread = dot(sel, tails)
    lane = iota((256, T), 1)
    block = (iota((256, T), 0) % T) // 8
    spread = jnp.where((lane == 64 + block) | (lane == 80 + block), spread, 0.0).astype(BF16)
    src, dst = iota((T, 256), 0), iota((T, 256), 1)
    gather = ((src >= 64) & (src < 80) & (dst < T)) | ((src >= 80) & (src < 96) & (dst >= T))
    both = dot(spread, gather.astype(BF16))
    order = both[:, :T].astype(I32)
    count = both[:, T:]
    count_ref[...] = count
    source = order >> 1
    source = ((source & (NZ - 1)) << 3) + (source >> 3)
    target = (source << 2) + ((iota((256, T), 0) >> 7) << 1) + (order & 1)
    perm = jnp.concatenate(
        [jnp.where(lane + T * m == target, 1.0, 0.0).astype(BF16) for m in range(2)], axis=1
    )
    top = iota((NP, 8, T), 1) < 4
    for copy in copies[1:]:
        copy.wait()
    tiles = [[] for _ in range(4)]
    for q in range(5):
        here = arrived_ref[:, pl.ds(16 * q, 16), :].astype(F32).reshape(NP, 2, 2, 8, T)
        for half in range(2):
            even, odd = here[:, 0, half], here[:, 1, half]
            low = jnp.where(top, even, pltpu.roll(odd, 4, 1))
            high = jnp.where(top, pltpu.roll(even, 4, 1), odd)
            tiles[2 * half].append(low.reshape(256, T))
            tiles[2 * half + 1].append(high.reshape(256, T))
    for j in range(4):
        rows = dot(perm, jnp.concatenate(tiles[j], axis=1).astype(BF16)).astype(BF16)
        for q in range(4):
            x_ref[:, pl.ds(T * (4 * q + j), T)] = rows[:, T * q : T * q + T]
        bc_ref[:, pl.ds(T * j, T)] = rows[:, T * 4 :]
    steps_in = arrived_ref[:, pl.ds(80, 8), :].astype(F32).reshape(512, T).astype(BF16)
    target = (source << 3) + (order & 1)
    small = jnp.concatenate(
        [jnp.where(lane + T * m == target, 1.0, 0.0).astype(BF16) for m in range(4)], axis=1
    )
    raw = dot(small, steps_in)
    first = iota((T, T), 1) < HH
    raw = jnp.where(first, raw[:T], raw[T:])
    cnt = jnp.where(first, count[:T], count[T:])
    step = softplus(raw)
    logd = -step * rate_ref[...]
    lower = (iota((T, T), 0) >= iota((T, T), 1)).astype(F32)
    cum = jnp.dot(lower, logd, preferred_element_type=F32, precision=lax.Precision.HIGHEST)
    cum_ref[...] = cum
    key_ref[...] = (cum - jnp.log(step)).T
    last = cum[T - 1 : T]
    last_cnt = cnt[T - 1 : T]
    entry = jnp.where(cnt == 0.0, jnp.exp(cum), 0.0)
    entry_ref[...] = entry
    decay = jnp.where(last_cnt == 0.0, jnp.exp(last), 0.0)
    decay = jnp.broadcast_to(decay, (8, T))
    before = jnp.where(iota((8, T), 1) < HH, 1.0, pltpu.roll(decay, HH, 1))
    carry_ref[...] = entry * before[:1]
    coef = two_parts(jnp.where(cnt == last_cnt, jnp.exp(last - cum) * step, 0.0))
    e = expander()
    decay = two_parts(decay)
    decay = dot(of_span(decay, 1), e)[:1]
    weighted = []
    for i in range(2):
        here = pl.ds(T * i, T)
        weighted.append((x_ref[here, :].astype(F32) * dot(of_span(coef, i), e)).astype(BF16))
    for tile in range(2):
        b = [bc_ref[pl.ds(T * i, T), pl.ds(T * tile, T)].astype(F32).T.astype(BF16) for i in range(2)]
        for half in range(2):
            g = 2 * tile + half
            lanes = slice(GW * g, GW * g + GW)
            states = [dot(b[i][N * half : N * half + N], weighted[i][:, lanes]) for i in range(2)]
            hin_ref[:, lanes] = states[0].astype(BF16)
            h = (decay[:, lanes] * states[0] + states[1]).astype(BF16)
            for pair in range(4):
                for k in range(2):
                    m = (4 * g + pair) * 2 + k
                    msg_ref[m, pl.ds(0, 32), :] = h[32 * k : 32 * k + 32, T * pair : T * pair + T]
    tails = arrived_ref[:, pl.ds(80, 8), :].astype(F32)
    sums_ref[...] = jnp.sum(tails, axis=0)
    chip, source = iota((NP, 512), 0), iota((NP, 512), 1) >> 3
    ends = ((source & (NZ - 1)) * NX + (source >> 4) == chip) & ((iota((NP, 512), 1) & 7) == 7)
    resets_ref[...] = dot(ends.astype(BF16), steps_in)


def local_kernel(
    x_ref, bc_ref, cum_ref, key_ref, entry_ref, carry_ref, count_ref, hin_ref, skip_ref,
    sums_ref, resets_ref, pair_ref, mine_ref, swap_ref, decay_ref, out_ref,
):
    core = lax.axis_index("c")
    there = pl.ds(pl.multiple_of(T * (1 - core), T), T)
    e = expander()
    entry = dot(of_span(two_parts(entry_ref[...]), 1), e)
    causal = iota((T, T), 0) >= iota((T, T), 1)
    left = iota((T, T), 1) < HP
    for i in range(2):
        here = pl.ds(T * i, T)
        count = count_ref[here, :]
        keep = causal & (count == count.T)
        for g in range(4):
            tile, half = g // 2, g % 2
            b = bc_ref[here, pl.ds(T * tile, T)][:, N * half : N * half + N]
            c = bc_ref[here, pl.ds(2 * T + T * tile, T)][:, N * half : N * half + N]
            scores = dot_nt(c, b)
            if i == 1:
                lanes = pl.ds(GW * g, GW)
                carried = dot(c, hin_ref[:, lanes]) * entry[:, GW * g : GW * g + GW]
            for pair in range(4):
                weights = []
                for h in (2 * pair, 2 * pair + 1):
                    col = HH * i + HG * g + h
                    gap = cum_ref[:, col : col + 1] - key_ref[col : col + 1, :]
                    weights.append((jnp.exp(jnp.where(keep, gap, -jnp.inf)) * scores).astype(BF16))
                lanes = pl.ds(GW * g + T * pair, T)
                x = x_ref[here, lanes]
                zero = jnp.zeros_like(x)
                both = jnp.concatenate([jnp.where(left, x, zero), jnp.where(left, zero, x)], axis=0)
                out = dot(jnp.concatenate(weights, axis=1), both) + skip_ref[:, lanes] * x.astype(F32)
                if i == 1:
                    out += carried[:, T * pair : T * pair + T]
                out_ref[here, lanes] = out
    mine_ref[...] = out_ref[pl.ds(pl.multiple_of(T * core, T), T), :]
    other = out_ref[there, :]
    high = other.astype(BF16)
    swap_ref[:, pl.ds(0, HW)] = high
    swap_ref[:, pl.ds(HW, HW)] = (other - high.astype(F32)).astype(BF16)
    swap_ref[:, pl.ds(2 * HW, 2 * T)] = bc_ref[there, pl.ds(2 * T, 2 * T)]
    swap_ref[:, pl.ds(2 * HW + 2 * T, T)] = of_span(two_parts(carry_ref[...]), 1 - core)
    sums = sums_ref[pl.ds(2, 2), :] + sums_ref[pl.ds(4, 2), :] + sums_ref[pl.ds(6, 2), :]
    sums = jnp.concatenate([sums, jnp.zeros((T - 2, T), F32)], axis=0).T[:NP]
    sums = jnp.where(iota((NP, T), 1) < HP, sums[:, 0:1], sums[:, 1:2])
    decay_ref[...] = jnp.where(resets_ref[:, 95:96] == 0.0, jnp.exp(-sums * pair_ref[...]), 0.0)


def scan_kernel(in_ref, decay_ref, out_ref):
    h = jnp.zeros((32, T), F32)
    for p in range(NP):
        at = (p % NX) * NZ + p // NX
        out_ref[at] = h.astype(BF16)
        h = decay_ref[pl.ds(p, 1), :] * h + in_ref[at].astype(F32)


def carried(c, h_ref, g, scale):
    state = jnp.concatenate(
        [jnp.concatenate([h_ref[8 * g + 2 * p], h_ref[8 * g + 2 * p + 1]], axis=0) for p in range(4)], axis=1
    )
    return dot(c, state) * scale[:, GW * g : GW * g + GW]


def mine_kernel(partial_ref, bc_ref, carry_ref, h_ref, out_ref):
    core = lax.axis_index("c")
    scale = dot(of_span(two_parts(carry_ref[...]), core), expander())
    cs = bc_ref[pl.ds(pl.multiple_of(T * core, T), T), pl.ds(2 * T, 2 * T)]
    for g in range(4):
        lanes = pl.ds(GW * g, GW)
        inter = carried(cs[:, N * g : N * g + N], h_ref, g, scale)
        out_ref[:, lanes] = (partial_ref[:, lanes] + inter).astype(BF16)


def final_kernel(mine_ref, swap_ref, h_ref, out_hbm, other_ref, sems):
    core = lax.axis_index("c")

    def copy(src, n, half):
        return pltpu.make_async_copy(src, out_hbm.at[:, pl.ds(HW * half, HW)], sems.at[n])

    for k in range(2):

        @pl.when(core == k)
        def _():
            copy(mine_ref, 0, k).start()

    scale = dot(swap_ref[:, pl.ds(2 * HW + 2 * T, T)], expander())
    cs = swap_ref[:, pl.ds(2 * HW, 2 * T)]
    for g in range(4):
        lanes = pl.ds(GW * g, GW)
        partial = swap_ref[:, lanes].astype(F32) + swap_ref[:, pl.ds(HW + GW * g, GW)].astype(F32)
        inter = carried(cs[:, N * g : N * g + N], h_ref, g, scale)
        other_ref[:, lanes] = (partial + inter).astype(BF16)
    for k in range(2):

        @pl.when(core == k)
        def _():
            copy(other_ref, 1, 1 - k).start()
            copy(mine_ref, 0, k).wait()
            copy(other_ref, 1, 1 - k).wait()


def per_device(x, b, c, dt, order, resets, rate, skip):
    core = lax.axis_index("c")
    sds = jax.ShapeDtypeStruct
    hbm = pl.BlockSpec(memory_space=pltpu.HBM)
    packed = pl.pallas_call(
        pack_kernel,
        out_shape=sds((2 * NX, NZ, MSG, T), BF16),
        in_specs=[hbm] * 6,
        out_specs=hbm,
        scratch_shapes=[
            pltpu.VMEM(x.shape, BF16),
            pltpu.VMEM(b.shape, BF16),
            pltpu.VMEM(c.shape, BF16),
            pltpu.VMEM(dt.shape[::-1], BF16),
            pltpu.VMEM((1, T), I32),
            pltpu.VMEM((1, T), I32),
            pltpu.VMEM((2 * NX, NZ, MSG, T), BF16),
            pltpu.SemaphoreType.DMA((3 + 3 * PARTS,)),
            pltpu.SemaphoreType.DMA((PARTS,)),
        ],
        compiler_params=params(56),
        name="pack",
    )(x, b, c, dt.T, order, resets.reshape(1, T))
    packed = packed.reshape(2 * NP, MSG, T)
    arrived = lax.all_to_all(packed, ("x", "c", "z"), split_axis=0, concat_axis=0, tiled=True)
    mine = lax.dynamic_slice_in_dim(rate, core * HH, HH)
    rate_row = jnp.concatenate([mine, mine, jnp.zeros((64,), F32)]).reshape(1, T)
    pair = (lax.axis_index("x") * NZ + lax.axis_index("z")) // 2 * 2
    pair_row = jnp.repeat(lax.dynamic_slice_in_dim(rate, core * HH + pair, 2), HP).reshape(1, T)
    skip_row = jnp.repeat(lax.dynamic_slice_in_dim(skip, core * HH, HH), HP).reshape(1, HW)
    xs, bc, cum, key, entry, carry, count, hin, msg, sums, ends = pl.pallas_call(
        state_kernel,
        out_shape=(
            sds((2 * T, HW), BF16),
            sds((2 * T, 4 * T), BF16),
            sds((T, T), F32),
            sds((T, T), F32),
            sds((T, T), F32),
            sds((T, T), F32),
            sds((2 * T, T), F32),
            sds((N, HW), BF16),
            sds((NP, 32, T), BF16),
            sds((8, T), F32),
            sds((NP, T), F32),
        ),
        in_specs=[hbm, pl.BlockSpec(memory_space=pltpu.VMEM)],
        scratch_shapes=[pltpu.VMEM((2 * NP, MSG, T), BF16), pltpu.SemaphoreType.DMA((2,))],
        compiler_params=params(51),
        name="state",
    )(arrived, rate_row)
    totals = lax.all_to_all(msg, ("x", "z"), split_axis=0, concat_axis=0, tiled=True)
    partial, swap, decays = pl.pallas_call(
        local_kernel,
        out_shape=(sds((T, HW), F32), sds((T, 2 * HW + 3 * T), BF16), sds((NP, T), F32)),
        scratch_shapes=[pltpu.VMEM((2 * T, HW), F32)],
        compiler_params=params(20),
        cost_estimate=pl.CostEstimate(flops=2_000_000_000, bytes_accessed=6_000_000, transcendentals=1_100_000),
        name="local",
    )(xs, bc, cum, key, entry, carry, count, hin, skip_row, sums, ends, pair_row)
    swap = lax.ppermute(swap, "c", [(0, 1), (1, 0)])
    entering = pl.pallas_call(
        scan_kernel, out_shape=sds((NP, 32, T), BF16), compiler_params=params(16), name="chips"
    )(totals, decays)
    states = lax.all_to_all(entering, ("x", "z"), split_axis=0, concat_axis=0, tiled=True)
    other = lax.ppermute(states, "c", [(0, 1), (1, 0)])
    own = pl.pallas_call(
        mine_kernel, out_shape=sds((T, HW), BF16), compiler_params=params(20), name="mine"
    )(partial, bc, carry, states)
    return pl.pallas_call(
        final_kernel,
        out_shape=sds((T, 2 * HW), BF16),
        in_specs=[pl.BlockSpec(memory_space=pltpu.VMEM)] * 3,
        out_specs=hbm,
        scratch_shapes=[pltpu.VMEM((T, HW), BF16), pltpu.SemaphoreType.DMA((2,))],
        compiler_params=params(20),
        name="final",
    )(own, swap, other)


def solution(mesh):
    fine = Mesh(mesh.devices.reshape(NZ, NX, 2, mesh.shape["seq"]), ("z", "x", "c", "seq"))
    rows = ("seq", "z", "x", "c")
    in_specs = (P(rows, None),) * 5 + (P(rows), P(), P())
    return jax.shard_map(
        per_device, mesh=fine, in_specs=in_specs, out_specs=P(rows, None), check_vma=False
    )
```

```python
import jax
import jax.numpy as jnp
from jax import lax
from jax.experimental import pallas as pl
from jax.experimental.pallas import tpu as pltpu
from jax.sharding import Mesh, PartitionSpec as P

F32 = jnp.float32
BF16 = jnp.bfloat16
I32 = jnp.int32
T = 128
NX, NZ = 4, 8
NP = NX * NZ
HG = 8
HP = 64
N = 64
GW = HG * HP
HH = 32
HW = HH * HP
MSG = 88
PARTS = 2
AWAY = 12288


def iota(shape, dim):
    return lax.broadcasted_iota(I32, shape, dim)


def dot(a, b):
    return jnp.dot(a, b, preferred_element_type=F32)


def dot_nt(a, b):
    return lax.dot_general(a, b, (((1,), (1,)), ((), ())), preferred_element_type=F32)


def params(mib):
    return pltpu.CompilerParams(vmem_limit_bytes=mib * 1024 * 1024)


def softplus(v):
    return jnp.maximum(v, 0.0) + jnp.log1p(jnp.exp(-jnp.abs(v)))


def three_parts(v):
    high = v.astype(BF16)
    rest = v - high.astype(F32)
    mid = rest.astype(BF16)
    return high, mid, (rest - mid.astype(F32)).astype(BF16)


def pack_kernel(
    x_hbm, b_hbm, c_hbm, dt_hbm, reset_hbm, out_hbm,
    x_ref, b_ref, c_ref, dt_ref, reset_ref, out_ref, sems, out_sems,
):
    pairs = [(reset_hbm, reset_ref), (dt_hbm, dt_ref)]
    span = T // PARTS
    for part in range(PARTS):
        rows = pl.ds(span * part, span)
        pairs += [(src.at[rows], dst.at[rows]) for src, dst in ((b_hbm, b_ref), (c_hbm, c_ref), (x_hbm, x_ref))]
    copies = [pltpu.make_async_copy(s, d, sems.at[n]) for n, (s, d) in enumerate(pairs)]
    for copy in copies:
        copy.start()
    row, col = iota((4 * span, 4 * span), 0), iota((4 * span, 4 * span), 1)
    pick = (col // span == (row % 16) // 4) & (col % span == (row // 16) * 4 + row % 4)
    pick = pick.astype(BF16)
    lane, head = iota((256, 64), 0), iota((256, 64), 1)
    spread = (lane % T < HH) & (head == (lane // T) * HH + lane % T)
    to, row = iota((256, T), 0), iota((256, T), 1)
    own_row = ((to % 8 < 4) & (row == (to // 8) * 4 + to % 8)).astype(BF16)
    to, head = iota((256, 64), 0), iota((256, 64), 1)
    chosen = ((to % 8 // 2 == 2) & (head == 2 * (to // 8) + to % 2)).astype(BF16)
    of_chip = (iota((T, T), 0) // 4 == iota((T, T), 1)).astype(BF16)
    chip = lax.axis_index("z") * NX + lax.axis_index("x")
    flag = (iota((8, T), 0) == 6) & (iota((8, T), 1) == chip)
    for copy in copies[:2]:
        copy.wait()
    dt = dt_ref[...]
    wide = dot(spread.astype(BF16), dt).astype(BF16)
    steps = dot_nt(own_row, wide)
    sums = dot(jnp.concatenate(three_parts(softplus(dt.astype(F32))), axis=0), of_chip)
    high, mid, low = three_parts(sums[:64] + sums[64:128] + sums[128:])
    sums = high.astype(F32) + pltpu.roll(mid.astype(F32), HH, 1) + pltpu.roll(low.astype(F32), 2 * HH, 1)
    sums = dot(chosen, sums.astype(BF16))
    resets = jnp.sum(reset_ref[...].astype(F32), axis=1, keepdims=True)
    flag = jnp.where(flag, jnp.broadcast_to(resets, (8, T)), 0.0)
    sent = []
    for part in range(PARTS):
        for copy in copies[2 + 3 * part : 5 + 3 * part]:
            copy.wait()
        rows = pl.ds(span * part, span)
        tiles = []
        for c in range(2):
            for q in range(4):
                tiles.append([x_ref[rows, pl.ds(HW * c + 512 * q + T * j, T)] for j in range(4)])
            tiles.append(
                [b_ref[rows, pl.ds(256 * c, T)], b_ref[rows, pl.ds(256 * c + T, T)],
                 c_ref[rows, pl.ds(256 * c, T)], c_ref[rows, pl.ds(256 * c + T, T)]]
            )
        right = jnp.concatenate([jnp.concatenate(t, axis=0) for t in tiles], axis=1)
        got = dot(pick, right).astype(BF16)
        for p in range(NP // PARTS):
            z, x = NZ // PARTS * part + p // NX, p % NX
            at = 8 * (NP // PARTS * part + p)
            for c in range(2):
                to = 2 * x + c
                for q in range(5):
                    lanes = slice(T * (5 * c + q), T * (5 * c + q) + T)
                    out_ref[to, z, pl.ds(16 * q, 16), :] = got[16 * p : 16 * p + 16, lanes]
                m = 8 * (16 * c + (NZ * x + z) // 2)
                tail = steps[at : at + 8, T * c : T * c + T] + sums[m : m + 8] + flag
                out_ref[to, z, pl.ds(80, 8), :] = tail.astype(BF16)
        here = pl.ds(NZ // PARTS * part, NZ // PARTS)
        sent.append(pltpu.make_async_copy(out_ref.at[:, here], out_hbm.at[:, here], out_sems.at[part]))
        sent[-1].start()
    for copy in sent:
        copy.wait()


def columns(row):
    return jnp.broadcast_to(row, (T, T)).T


def plan_kernel(order_ref, order2_ref, reset_ref, reset2_ref, perm_ref, cnt_ref):
    core = lax.axis_index("c")
    orders = [order_ref[...].astype(F32), order2_ref[...].astype(F32)]
    resets = [reset_ref[...].astype(F32), reset2_ref[...].astype(F32)]
    orders = [columns(jnp.where(core == i, orders[0], orders[1])) for i in range(2)]
    upto = (iota((T, T), 0) <= iota((T, T), 1)).astype(BF16)
    counts = []
    for i in range(2):
        row = jnp.broadcast_to(jnp.where(core == i, resets[0], resets[1]), (8, T))
        counts.append(columns(dot(row.astype(BF16), upto)[:1]))
    cnt_ref[...] = jnp.where(iota((T, T), 1) < HH, counts[0], counts[1])
    order = jnp.concatenate(orders, axis=0).astype(I32)
    source = order >> 1
    source = ((source & (NZ - 1)) << 3) + (source >> 3)
    target = (source << 2) + ((iota((256, T), 0) >> 7) << 1) + (order & 1)
    for m in range(2):
        perm_ref[:, pl.ds(T * m, T)] = jnp.where(iota((256, T), 1) + T * m == target, 1.0, 0.0).astype(BF16)


def expander():
    gap = iota((T, T), 0) % HH - iota((T, T), 1) // HP
    return jnp.concatenate([jnp.where(gap == 2 * t, 1.0, 0.0).astype(BF16) for t in range(HW // T)], axis=1)


def two_parts(v):
    high = v.astype(BF16).astype(F32)
    low = v - high
    return jnp.where(iota(v.shape, 1) < 64, high, pltpu.roll(low, 64, 1))


def of_span(parts, i):
    return jnp.where((iota(parts.shape, 1) % 64) // HH == i, parts, 0.0).astype(BF16)


def inner_weights(cum, step, cnt):
    last, last_cnt = cum[T - 1 : T], cnt[T - 1 : T]
    return two_parts(jnp.where(cnt == last_cnt, jnp.exp(last - cum) * step, 0.0))


def span_decay(cum, cnt):
    return jnp.where(cnt[T - 1 : T] == 0.0, jnp.exp(cum[T - 1 : T]), 0.0)


def x_tile(x_ref, rows, t):
    return x_ref[rows, pl.ds(T * (4 * (t % 4) + t // 4), T)]


def state_kernel(
    arrived_ref, rate_ref, perm_ref, cnt_ref, x_hbm, bc_ref, cum_ref, step_ref, msg_ref, sums_ref, x_ref, x_sems
):
    top = iota((NP, 8, T), 1) < 4

    def halves(here):
        even, odd = here[:, 0], here[:, 1]
        low = jnp.where(top, even, pltpu.roll(odd, 4, 1)).reshape(256, T).astype(BF16)
        high = jnp.where(top, pltpu.roll(even, 4, 1), odd).reshape(256, T).astype(BF16)
        return low, high

    perm = perm_ref[...]
    cnt = cnt_ref[...]
    tails = arrived_ref[:, pl.ds(80, 8), :].astype(F32)
    sums_ref[...] = jnp.sum(tails, axis=0)
    raw = dot(perm, halves(tails.reshape(NP, 2, 8, T))[0])
    raw = jnp.where(iota((T, T), 1) < HH, raw[:T], pltpu.roll(raw[T:], HH, 1))
    step = softplus(raw)
    lower = (iota((T, T), 0) >= iota((T, T), 1)).astype(BF16)
    cum = dot(lower, jnp.concatenate(three_parts(-step * rate_ref[...]), axis=1))
    cum = cum[:, :T] + cum[:, T : 2 * T] + cum[:, 2 * T :]
    cum_ref[...] = cum
    step_ref[...] = step
    tiles = [[] for _ in range(4)]
    for q in range(5):
        here = arrived_ref[:, pl.ds(16 * q, 16), :].astype(F32).reshape(NP, 2, 2, 8, T)
        for half in range(2):
            low, high = halves(here[:, :, half])
            tiles[2 * half].append(low)
            tiles[2 * half + 1].append(high)
    x_copies = []
    for j in range(4):
        rows = dot(perm, jnp.concatenate(tiles[j], axis=1)).astype(BF16)
        here = pl.ds(GW * j, GW)
        x_ref[:, here] = rows[:, :GW]
        bc_ref[:, pl.ds(T * j, T)] = rows[:, GW:]
        x_copies.append(pltpu.make_async_copy(x_ref.at[:, here], x_hbm.at[pl.ds(0, 2 * T), here], x_sems.at[j]))
        x_copies[-1].start()
    e = expander()
    coef = inner_weights(cum, step, cnt)
    decay = two_parts(jnp.broadcast_to(span_decay(cum, cnt), (8, T)))
    decay = dot(of_span(decay, 1), e)[:1]
    weighted = []
    for i in range(2):
        here = pl.ds(T * i, T)
        scale = dot(of_span(coef, i), e)
        weighted.append([(x_tile(x_ref, here, t).astype(F32) * scale[:, T * t : T * t + T]).astype(BF16) for t in range(16)])
    for tile in range(2):
        b = [bc_ref[pl.ds(T * i, T), pl.ds(T * tile, T)].astype(F32).T.astype(BF16) for i in range(2)]
        for half in range(2):
            g = 2 * tile + half
            lanes = slice(GW * g, GW * g + GW)
            states = [dot(b[i][N * half : N * half + N], jnp.concatenate(weighted[i][4 * g : 4 * g + 4], axis=1)) for i in range(2)]
            h = (decay[:, lanes] * states[0] + states[1]).astype(BF16)
            for pair in range(4):
                for k in range(2):
                    m = (4 * g + pair) * 2 + k
                    msg_ref[m] = h[32 * k : 32 * k + 32, T * pair : T * pair + T]
    for copy in x_copies:
        copy.wait()


def local_kernel(
    x_hbm, bc_ref, cum_ref, step_ref, cnt_ref, skip_ref, sums_ref, pair_ref,
    mine_ref, factor_ref, swap_ref, decay_ref, out_ref, key_ref, x_ref, x_sem,
):
    x_copy = pltpu.make_async_copy(x_hbm.at[pl.ds(0, 2 * T)], x_ref, x_sem)
    x_copy.start()
    core = lax.axis_index("c")
    there = pl.ds(pl.multiple_of(T * (1 - core), T), T)
    cum, step, cnt = cum_ref[...], step_ref[...], cnt_ref[...]
    key_ref[...] = (cum - jnp.log(step)).T
    entry = jnp.where(cnt == 0.0, jnp.exp(cum), 0.0)
    decay = jnp.broadcast_to(span_decay(cum, cnt), (8, T))
    before = jnp.where(iota((8, T), 1) < HH, 1.0, pltpu.roll(decay, HH, 1))
    carry = two_parts(entry * before[:1])
    factor_ref[...] = of_span(carry, core)
    e = expander()
    entry = dot(of_span(two_parts(entry), 1), e)
    x_copy.wait()
    inner = dot(of_span(inner_weights(cum, step, cnt), 0), e)
    weighted = [
        (x_tile(x_ref, pl.ds(0, T), t).astype(F32) * inner[:, T * t : T * t + T]).astype(BF16) for t in range(16)
    ]
    causal = iota((T, T), 0) >= iota((T, T), 1)
    left = iota((T, T), 1) < HP
    for i in range(2):
        here = pl.ds(T * i, T)
        count = jnp.broadcast_to(cnt[:, HH * i : HH * i + 1], (T, T))
        keep = causal & (count == count.T)
        for g in range(4):
            tile, half = g // 2, g % 2
            b = bc_ref[here, pl.ds(T * tile, T)][:, N * half : N * half + N]
            c = bc_ref[here, pl.ds(2 * T + T * tile, T)][:, N * half : N * half + N]
            scores = dot_nt(c, b)
            if i == 1:
                lanes = slice(GW * g, GW * g + GW)
                first = bc_ref[pl.ds(0, T), pl.ds(T * tile, T)].astype(F32).T[N * half : N * half + N].astype(BF16)
                state = dot(first, jnp.concatenate(weighted[4 * g : 4 * g + 4], axis=1)).astype(BF16)
                carried = dot(c, state) * entry[:, lanes]
            for pair in range(4):
                weights = []
                for h in (2 * pair, 2 * pair + 1):
                    col = HH * i + HG * g + h
                    gap = cum_ref[:, col : col + 1] - key_ref[col : col + 1, :]
                    weights.append((jnp.exp(jnp.where(keep, gap, -jnp.inf)) * scores).astype(BF16))
                lanes = pl.ds(GW * g + T * pair, T)
                x = x_tile(x_ref, here, 4 * g + pair)
                zero = jnp.zeros_like(x)
                both = jnp.concatenate([jnp.where(left, x, zero), jnp.where(left, zero, x)], axis=0)
                out = dot(jnp.concatenate(weights, axis=1), both) + skip_ref[:, lanes] * x.astype(F32)
                if i == 1:
                    out += carried[:, T * pair : T * pair + T]
                out_ref[here, lanes] = out
    mine_ref[...] = out_ref[pl.ds(pl.multiple_of(T * core, T), T), :]
    other = out_ref[there, :]
    high = other.astype(BF16)
    swap_ref[:, pl.ds(0, HW)] = high
    swap_ref[:, pl.ds(HW, HW)] = (other - high.astype(F32)).astype(BF16)
    swap_ref[:, pl.ds(2 * HW, 2 * T)] = bc_ref[there, pl.ds(2 * T, 2 * T)]
    swap_ref[:, pl.ds(2 * HW + 2 * T, T)] = of_span(carry, 1 - core)
    tails = sums_ref[...]
    sums = tails + pltpu.roll(tails, T - HH, 1) + pltpu.roll(tails, T - 2 * HH, 1)
    rows = iota((8, T), 0)
    sums = jnp.where(rows == 6, tails, sums)
    sums = jnp.concatenate([sums, jnp.zeros((T - 8, T), F32)], axis=0).T[:NP]
    resets = sums[:, 6:7]
    sums = jnp.where(iota((NP, T), 1) < HP, sums[:, 4:5], sums[:, 5:6])
    decay_ref[...] = jnp.where(resets == 0.0, jnp.exp(-sums * pair_ref[...]), 0.0)


def scan_kernel(in_ref, decay_ref, out_ref):
    h = jnp.zeros((32, T), F32)
    for p in range(NP):
        at = (p % NX) * NZ + p // NX
        out_ref[at] = h.astype(BF16)
        h = decay_ref[pl.ds(p, 1), :] * h + in_ref[at].astype(F32)


def carried(c, h_ref, g, scale):
    state = jnp.concatenate(
        [jnp.concatenate([h_ref[8 * g + 2 * p], h_ref[8 * g + 2 * p + 1]], axis=0) for p in range(4)], axis=1
    )
    return dot(c, state) * scale[:, GW * g : GW * g + GW]


def mine_kernel(partial_ref, bc_ref, factor_ref, h_ref, out_ref):
    core = lax.axis_index("c")
    scale = dot(factor_ref[...], expander())
    cs = bc_ref[pl.ds(pl.multiple_of(T * core, T), T), pl.ds(2 * T, 2 * T)]
    for g in range(4):
        lanes = pl.ds(GW * g, GW)
        inter = carried(cs[:, N * g : N * g + N], h_ref, g, scale)
        out_ref[:, lanes] = (partial_ref[:, lanes] + inter).astype(BF16)


def final_kernel(mine_ref, swap_ref, h_ref, out_hbm, other_ref, sems):
    core = lax.axis_index("c")

    def copy(src, n, half):
        return pltpu.make_async_copy(src, out_hbm.at[:, pl.ds(HW * half, HW)], sems.at[n])

    for k in range(2):

        @pl.when(core == k)
        def _():
            copy(mine_ref, 0, k).start()

    scale = dot(swap_ref[:, pl.ds(2 * HW + 2 * T, T)], expander())
    cs = swap_ref[:, pl.ds(2 * HW, 2 * T)]
    for g in range(4):
        lanes = pl.ds(GW * g, GW)
        partial = swap_ref[:, lanes].astype(F32) + swap_ref[:, pl.ds(HW + GW * g, GW)].astype(F32)
        inter = carried(cs[:, N * g : N * g + N], h_ref, g, scale)
        other_ref[:, lanes] = (partial + inter).astype(BF16)
    for k in range(2):

        @pl.when(core == k)
        def _():
            copy(other_ref, 1, 1 - k).start()
            copy(mine_ref, 0, k).wait()
            copy(other_ref, 1, 1 - k).wait()


def per_device(x, b, c, dt, order, resets, rate, skip):
    core = lax.axis_index("c")
    sds = jax.ShapeDtypeStruct
    hbm, vmem = pl.BlockSpec(memory_space=pltpu.HBM), pl.BlockSpec(memory_space=pltpu.VMEM)
    resets = resets.reshape(1, T)
    packed = pl.pallas_call(
        pack_kernel,
        out_shape=sds((2 * NX, NZ, MSG, T), BF16),
        in_specs=[hbm] * 5,
        out_specs=hbm,
        scratch_shapes=[
            pltpu.VMEM(x.shape, BF16),
            pltpu.VMEM(b.shape, BF16),
            pltpu.VMEM(c.shape, BF16),
            pltpu.VMEM(dt.shape[::-1], BF16),
            pltpu.VMEM((1, T), I32),
            pltpu.VMEM((2 * NX, NZ, MSG, T), BF16),
            pltpu.SemaphoreType.DMA((2 + 3 * PARTS,)),
            pltpu.SemaphoreType.DMA((PARTS,)),
        ],
        compiler_params=params(56),
        name="pack",
    )(x, b, c, dt.T, resets)
    packed = packed.reshape(2 * NP, MSG, T)
    arrived = lax.all_to_all(packed, ("x", "c", "z"), split_axis=0, concat_axis=0, tiled=True)
    order2 = lax.ppermute(order, "c", [(0, 1), (1, 0)])
    resets2 = lax.ppermute(resets, "c", [(0, 1), (1, 0)])
    perm, cnt = pl.pallas_call(
        plan_kernel,
        out_shape=(sds((2 * T, 2 * T), BF16), sds((T, T), F32)),
        compiler_params=params(16),
        cost_estimate=pl.CostEstimate(flops=1_000_000_000, bytes_accessed=1_000_000, transcendentals=0),
        name="plan",
    )(order, order2, resets, resets2)
    mine = lax.dynamic_slice_in_dim(rate, core * HH, HH)
    rate_row = jnp.concatenate([mine, mine, jnp.zeros((64,), F32)]).reshape(1, T)
    pair = (lax.axis_index("x") * NZ + lax.axis_index("z")) // 2 * 2
    pair_row = jnp.repeat(lax.dynamic_slice_in_dim(rate, core * HH + pair, 2), HP).reshape(1, T)
    skip_row = jnp.repeat(lax.dynamic_slice_in_dim(skip, core * HH, HH), HP).reshape(1, HW)
    xs, bc, cum, step, msg, sums = pl.pallas_call(
        state_kernel,
        out_shape=(
            sds((AWAY, HW), BF16),
            sds((2 * T, 4 * T), BF16),
            sds((T, T), F32),
            sds((T, T), F32),
            sds((NP, 32, T), BF16),
            sds((8, T), F32),
        ),
        out_specs=(hbm,) + (vmem,) * 5,
        scratch_shapes=[pltpu.VMEM((2 * T, HW), BF16), pltpu.SemaphoreType.DMA((4,))],
        compiler_params=params(24),
        name="state",
    )(arrived, rate_row, perm, cnt)
    totals = lax.all_to_all(msg, ("x", "z"), split_axis=0, concat_axis=0, tiled=True)
    partial, factors, swap, decays = pl.pallas_call(
        local_kernel,
        out_shape=(sds((T, HW), F32), sds((T, T), BF16), sds((T, 2 * HW + 3 * T), BF16), sds((NP, T), F32)),
        in_specs=[hbm] + [vmem] * 7,
        scratch_shapes=[
            pltpu.VMEM((2 * T, HW), F32),
            pltpu.VMEM((T, T), F32),
            pltpu.VMEM((2 * T, HW), BF16),
            pltpu.SemaphoreType.DMA,
        ],
        compiler_params=params(20),
        cost_estimate=pl.CostEstimate(flops=2_000_000_000, bytes_accessed=6_000_000, transcendentals=1_100_000),
        name="local",
    )(xs, bc, cum, step, cnt, skip_row, sums, pair_row)
    swap = lax.ppermute(swap, "c", [(0, 1), (1, 0)])
    entering = pl.pallas_call(
        scan_kernel, out_shape=sds((NP, 32, T), BF16), compiler_params=params(16), name="chips"
    )(totals, decays)
    states = lax.all_to_all(entering, ("x", "z"), split_axis=0, concat_axis=0, tiled=True)
    other = lax.ppermute(states, "c", [(0, 1), (1, 0)])
    own = pl.pallas_call(
        mine_kernel, out_shape=sds((T, HW), BF16), compiler_params=params(20), name="mine"
    )(partial, bc, factors, states)
    return pl.pallas_call(
        final_kernel,
        out_shape=sds((T, 2 * HW), BF16),
        in_specs=[pl.BlockSpec(memory_space=pltpu.VMEM)] * 3,
        out_specs=hbm,
        scratch_shapes=[pltpu.VMEM((T, HW), BF16), pltpu.SemaphoreType.DMA((2,))],
        compiler_params=params(20),
        name="final",
    )(own, swap, other)


def solution(mesh):
    fine = Mesh(mesh.devices.reshape(NZ, NX, 2, mesh.shape["seq"]), ("z", "x", "c", "seq"))
    rows = ("seq", "z", "x", "c")
    in_specs = (P(rows, None),) * 5 + (P(rows), P(), P())
    return jax.shard_map(
        per_device, mesh=fine, in_specs=in_specs, out_specs=P(rows, None), check_vma=False
    )
```

```python
import jax
import jax.numpy as jnp
from jax import lax
from jax.experimental import pallas as pl
from jax.experimental.pallas import tpu as pltpu
from jax.sharding import Mesh, PartitionSpec as P

F32 = jnp.float32
BF16 = jnp.bfloat16
I32 = jnp.int32
T = 128
NX, NZ = 4, 8
NP = NX * NZ
HG = 8
HP = 64
N = 64
GW = HG * HP
HH = 32
HW = HH * HP
MSG = 88
PARTS = 2
AWAY = 12288


def iota(shape, dim):
    return lax.broadcasted_iota(I32, shape, dim)


def dot(a, b):
    return jnp.dot(a, b, preferred_element_type=F32)


def dot_nt(a, b):
    return lax.dot_general(a, b, (((1,), (1,)), ((), ())), preferred_element_type=F32)


def params(mib):
    return pltpu.CompilerParams(vmem_limit_bytes=mib * 1024 * 1024)


def softplus(v):
    return jnp.maximum(v, 0.0) + jnp.log1p(jnp.exp(-jnp.abs(v)))


def three_parts(v):
    high = v.astype(BF16)
    rest = v - high.astype(F32)
    mid = rest.astype(BF16)
    return high, mid, (rest - mid.astype(F32)).astype(BF16)


def pack_kernel(
    x_hbm, b_hbm, c_hbm, dt_hbm, reset_hbm, out_hbm,
    x_ref, b_ref, c_ref, dt_ref, reset_ref, out_ref, sems, out_sems,
):
    pairs = [(reset_hbm, reset_ref), (dt_hbm, dt_ref)]
    span = T // PARTS
    for part in range(PARTS):
        rows = pl.ds(span * part, span)
        pairs += [(src.at[rows], dst.at[rows]) for src, dst in ((b_hbm, b_ref), (c_hbm, c_ref), (x_hbm, x_ref))]
    copies = [pltpu.make_async_copy(s, d, sems.at[n]) for n, (s, d) in enumerate(pairs)]
    for copy in copies:
        copy.start()
    row, col = iota((4 * span, 4 * span), 0), iota((4 * span, 4 * span), 1)
    pick = (col // span == (row % 16) // 4) & (col % span == (row // 16) * 4 + row % 4)
    pick = pick.astype(BF16)
    lane, head = iota((256, 64), 0), iota((256, 64), 1)
    spread = (lane % T < HH) & (head == (lane // T) * HH + lane % T)
    to, row = iota((256, T), 0), iota((256, T), 1)
    own_row = ((to % 8 < 4) & (row == (to // 8) * 4 + to % 8)).astype(BF16)
    to, head = iota((256, 64), 0), iota((256, 64), 1)
    chosen = ((to % 8 // 2 == 2) & (head == 2 * (to // 8) + to % 2)).astype(BF16)
    of_chip = (iota((T, T), 0) // 4 == iota((T, T), 1)).astype(BF16)
    chip = lax.axis_index("z") * NX + lax.axis_index("x")
    flag = (iota((8, T), 0) == 6) & (iota((8, T), 1) == chip)
    for copy in copies[:2]:
        copy.wait()
    dt = dt_ref[...]
    wide = dot(spread.astype(BF16), dt).astype(BF16)
    steps = dot_nt(own_row, wide)
    sums = dot(jnp.concatenate(three_parts(softplus(dt.astype(F32))), axis=0), of_chip)
    high, mid, low = three_parts(sums[:64] + sums[64:128] + sums[128:])
    sums = high.astype(F32) + pltpu.roll(mid.astype(F32), HH, 1) + pltpu.roll(low.astype(F32), 2 * HH, 1)
    sums = dot(chosen, sums.astype(BF16))
    resets = jnp.sum(reset_ref[...].astype(F32), axis=1, keepdims=True)
    flag = jnp.where(flag, jnp.broadcast_to(resets, (8, T)), 0.0)
    sent = []
    for part in range(PARTS):
        for copy in copies[2 + 3 * part : 5 + 3 * part]:
            copy.wait()
        rows = pl.ds(span * part, span)
        tiles = []
        for c in range(2):
            for q in range(4):
                tiles.append([x_ref[rows, pl.ds(HW * c + 512 * q + T * j, T)] for j in range(4)])
            tiles.append(
                [b_ref[rows, pl.ds(256 * c, T)], b_ref[rows, pl.ds(256 * c + T, T)],
                 c_ref[rows, pl.ds(256 * c, T)], c_ref[rows, pl.ds(256 * c + T, T)]]
            )
        right = jnp.concatenate([jnp.concatenate(t, axis=0) for t in tiles], axis=1)
        got = dot(pick, right).astype(BF16)
        for p in range(NP // PARTS):
            z, x = NZ // PARTS * part + p // NX, p % NX
            at = 8 * (NP // PARTS * part + p)
            for c in range(2):
                to = 2 * x + c
                for q in range(5):
                    lanes = slice(T * (5 * c + q), T * (5 * c + q) + T)
                    out_ref[to, z, pl.ds(16 * q, 16), :] = got[16 * p : 16 * p + 16, lanes]
                m = 8 * (16 * c + (NZ * x + z) // 2)
                tail = steps[at : at + 8, T * c : T * c + T] + sums[m : m + 8] + flag
                out_ref[to, z, pl.ds(80, 8), :] = tail.astype(BF16)
        here = pl.ds(NZ // PARTS * part, NZ // PARTS)
        sent.append(pltpu.make_async_copy(out_ref.at[:, here], out_hbm.at[:, here], out_sems.at[part]))
        sent[-1].start()
    for copy in sent:
        copy.wait()


def columns(row):
    return jnp.broadcast_to(row, (T, T)).T


def plan_kernel(order_ref, order2_ref, reset_ref, reset2_ref, perm_ref, cnt_ref):
    core = lax.axis_index("c")
    orders = [order_ref[...].astype(F32), order2_ref[...].astype(F32)]
    resets = [reset_ref[...].astype(F32), reset2_ref[...].astype(F32)]
    orders = [columns(jnp.where(core == i, orders[0], orders[1])) for i in range(2)]
    upto = (iota((T, T), 0) <= iota((T, T), 1)).astype(BF16)
    counts = []
    for i in range(2):
        row = jnp.broadcast_to(jnp.where(core == i, resets[0], resets[1]), (8, T))
        counts.append(columns(dot(row.astype(BF16), upto)[:1]))
    cnt_ref[...] = jnp.where(iota((T, T), 1) < HH, counts[0], counts[1])
    order = jnp.concatenate(orders, axis=0).astype(I32)
    source = order >> 1
    source = ((source & (NZ - 1)) << 3) + (source >> 3)
    target = (source << 2) + ((iota((256, T), 0) >> 7) << 1) + (order & 1)
    for m in range(2):
        perm_ref[:, pl.ds(T * m, T)] = jnp.where(iota((256, T), 1) + T * m == target, 1.0, 0.0).astype(BF16)


def expander():
    gap = iota((T, T), 0) % HH - iota((T, T), 1) // HP
    return jnp.concatenate([jnp.where(gap == 2 * t, 1.0, 0.0).astype(BF16) for t in range(HW // T)], axis=1)


def two_parts(v):
    high = v.astype(BF16).astype(F32)
    low = v - high
    return jnp.where(iota(v.shape, 1) < 64, high, pltpu.roll(low, 64, 1))


def of_span(parts, i):
    return jnp.where((iota(parts.shape, 1) % 64) // HH == i, parts, 0.0).astype(BF16)


def inner_weights(cum, step, cnt):
    last, last_cnt = cum[T - 1 : T], cnt[T - 1 : T]
    return two_parts(jnp.where(cnt == last_cnt, jnp.exp(last - cum) * step, 0.0))


def span_decay(cum, cnt):
    return jnp.where(cnt[T - 1 : T] == 0.0, jnp.exp(cum[T - 1 : T]), 0.0)


def x_tile(x_ref, rows, t):
    return x_ref[rows, pl.ds(T * (4 * (t % 4) + t // 4), T)]


def state_kernel(
    arrived_ref, rate_ref, perm_ref, cnt_ref, x_hbm, bc_ref, cum_ref, step_ref, msg_hbm, sums_ref, x_ref, x_sems, msg_ref, msg_sems
):
    top = iota((NP, 8, T), 1) < 4

    def halves(here):
        even, odd = here[:, 0], here[:, 1]
        low = jnp.where(top, even, pltpu.roll(odd, 4, 1)).reshape(256, T).astype(BF16)
        high = jnp.where(top, pltpu.roll(even, 4, 1), odd).reshape(256, T).astype(BF16)
        return low, high

    perm = perm_ref[...]
    cnt = cnt_ref[...]
    tails = arrived_ref[:, pl.ds(80, 8), :].astype(F32)
    sums_ref[...] = jnp.sum(tails, axis=0)
    raw = dot(perm, halves(tails.reshape(NP, 2, 8, T))[0])
    raw = jnp.where(iota((T, T), 1) < HH, raw[:T], pltpu.roll(raw[T:], HH, 1))
    step = softplus(raw)
    lower = (iota((T, T), 0) >= iota((T, T), 1)).astype(BF16)
    cum = dot(lower, jnp.concatenate(three_parts(-step * rate_ref[...]), axis=1))
    cum = cum[:, :T] + cum[:, T : 2 * T] + cum[:, 2 * T :]
    cum_ref[...] = cum
    step_ref[...] = step
    tiles = [[] for _ in range(4)]
    for q in range(5):
        here = arrived_ref[:, pl.ds(16 * q, 16), :].astype(F32).reshape(NP, 2, 2, 8, T)
        for half in range(2):
            low, high = halves(here[:, :, half])
            tiles[2 * half].append(low)
            tiles[2 * half + 1].append(high)
    x_copies = []
    for j in range(4):
        rows = dot(perm, jnp.concatenate(tiles[j], axis=1)).astype(BF16)
        here = pl.ds(GW * j, GW)
        x_ref[:, here] = rows[:, :GW]
        bc_ref[:, pl.ds(T * j, T)] = rows[:, GW:]
        x_copies.append(pltpu.make_async_copy(x_ref.at[:, here], x_hbm.at[pl.ds(0, 2 * T), here], x_sems.at[j]))
        x_copies[-1].start()
    e = expander()
    coef = inner_weights(cum, step, cnt)
    decay = two_parts(jnp.broadcast_to(span_decay(cum, cnt), (8, T)))
    decay = dot(of_span(decay, 1), e)[:1]
    weighted = []
    for i in range(2):
        here = pl.ds(T * i, T)
        scale = dot(of_span(coef, i), e)
        weighted.append([(x_tile(x_ref, here, t).astype(F32) * scale[:, T * t : T * t + T]).astype(BF16) for t in range(16)])
    for tile in range(2):
        b = [bc_ref[pl.ds(T * i, T), pl.ds(T * tile, T)].astype(F32).T.astype(BF16) for i in range(2)]
        for half in range(2):
            g = 2 * tile + half
            lanes = slice(GW * g, GW * g + GW)
            states = [dot(b[i][N * half : N * half + N], jnp.concatenate(weighted[i][4 * g : 4 * g + 4], axis=1)) for i in range(2)]
            h = (decay[:, lanes] * states[0] + states[1]).astype(BF16)
            for pair in range(4):
                for k in range(2):
                    m = (4 * g + pair) * 2 + k
                    msg_ref[m] = h[32 * k : 32 * k + 32, T * pair : T * pair + T]
            part = pl.ds(8 * g, 8)
            x_copies.append(pltpu.make_async_copy(msg_ref.at[part], msg_hbm.at[part], msg_sems.at[g]))
            x_copies[-1].start()
    for copy in x_copies:
        copy.wait()


def local_kernel(
    x_hbm, bc_ref, cum_ref, step_ref, cnt_ref, skip_ref, sums_ref, pair_ref,
    mine_ref, factor_ref, swap_ref, decay_ref, out_ref, key_ref, x_ref, x_sem,
):
    x_copy = pltpu.make_async_copy(x_hbm.at[pl.ds(0, 2 * T)], x_ref, x_sem)
    x_copy.start()
    core = lax.axis_index("c")
    there = pl.ds(pl.multiple_of(T * (1 - core), T), T)
    cum, step, cnt = cum_ref[...], step_ref[...], cnt_ref[...]
    key_ref[...] = (cum - jnp.log(step)).T
    entry = jnp.where(cnt == 0.0, jnp.exp(cum), 0.0)
    decay = jnp.broadcast_to(span_decay(cum, cnt), (8, T))
    before = jnp.where(iota((8, T), 1) < HH, 1.0, pltpu.roll(decay, HH, 1))
    carry = two_parts(entry * before[:1])
    factor_ref[...] = of_span(carry, core)
    e = expander()
    entry = dot(of_span(two_parts(entry), 1), e)
    causal = iota((T, T), 0) >= iota((T, T), 1)
    keeps, scores = [], []
    for i in range(2):
        here = pl.ds(T * i, T)
        count = jnp.broadcast_to(cnt[:, HH * i : HH * i + 1], (T, T))
        keeps.append(causal & (count == count.T))
        for g in range(4):
            lanes = slice(N * (g % 2), N * (g % 2) + N)
            b = bc_ref[here, pl.ds(T * (g // 2), T)][:, lanes]
            c = bc_ref[here, pl.ds(2 * T + T * (g // 2), T)][:, lanes]
            scores.append(dot_nt(c, b))
    x_copy.wait()
    inner = dot(of_span(inner_weights(cum, step, cnt), 0), e)
    weighted = [
        (x_tile(x_ref, pl.ds(0, T), t).astype(F32) * inner[:, T * t : T * t + T]).astype(BF16) for t in range(16)
    ]
    left = iota((T, T), 1) < HP
    for i in range(2):
        here = pl.ds(T * i, T)
        for g in range(4):
            tile, half = g // 2, g % 2
            if i == 1:
                c = bc_ref[here, pl.ds(2 * T + T * tile, T)][:, N * half : N * half + N]
                lanes = slice(GW * g, GW * g + GW)
                first = bc_ref[pl.ds(0, T), pl.ds(T * tile, T)].astype(F32).T[N * half : N * half + N].astype(BF16)
                state = dot(first, jnp.concatenate(weighted[4 * g : 4 * g + 4], axis=1)).astype(BF16)
                carried = dot(c, state) * entry[:, lanes]
            for pair in range(4):
                weights = []
                for h in (2 * pair, 2 * pair + 1):
                    col = HH * i + HG * g + h
                    gap = cum_ref[:, col : col + 1] - key_ref[col : col + 1, :]
                    weights.append((jnp.exp(jnp.where(keeps[i], gap, -jnp.inf)) * scores[4 * i + g]).astype(BF16))
                lanes = pl.ds(GW * g + T * pair, T)
                x = x_tile(x_ref, here, 4 * g + pair)
                zero = jnp.zeros_like(x)
                both = jnp.concatenate([jnp.where(left, x, zero), jnp.where(left, zero, x)], axis=0)
                out = dot(jnp.concatenate(weights, axis=1), both) + skip_ref[:, lanes] * x.astype(F32)
                if i == 1:
                    out += carried[:, T * pair : T * pair + T]
                out_ref[here, lanes] = out
    mine_ref[...] = out_ref[pl.ds(pl.multiple_of(T * core, T), T), :]
    other = out_ref[there, :]
    high = other.astype(BF16)
    swap_ref[:, pl.ds(0, HW)] = high
    swap_ref[:, pl.ds(HW, HW)] = (other - high.astype(F32)).astype(BF16)
    swap_ref[:, pl.ds(2 * HW, 2 * T)] = bc_ref[there, pl.ds(2 * T, 2 * T)]
    swap_ref[:, pl.ds(2 * HW + 2 * T, T)] = of_span(carry, 1 - core)
    tails = sums_ref[...]
    sums = tails + pltpu.roll(tails, T - HH, 1) + pltpu.roll(tails, T - 2 * HH, 1)
    rows = iota((8, T), 0)
    sums = jnp.where(rows == 6, tails, sums)
    sums = jnp.concatenate([sums, jnp.zeros((T - 8, T), F32)], axis=0).T[:NP]
    resets = sums[:, 6:7]
    sums = jnp.where(iota((NP, T), 1) < HP, sums[:, 4:5], sums[:, 5:6])
    decay_ref[...] = jnp.where(resets == 0.0, jnp.exp(-sums * pair_ref[...]), 0.0)


def scan_kernel(in_ref, decay_ref, out_ref):
    h = jnp.zeros((32, T), F32)
    for p in range(NP):
        at = (p % NX) * NZ + p // NX
        out_ref[at] = h.astype(BF16)
        h = decay_ref[pl.ds(p, 1), :] * h + in_ref[at].astype(F32)


def entering(h_ref, g):
    return jnp.concatenate(
        [jnp.concatenate([h_ref[8 * g + 2 * p], h_ref[8 * g + 2 * p + 1]], axis=0) for p in range(4)], axis=1
    )


def mine_kernel(partial_ref, bc_ref, factor_ref, h_ref, swap_ref, out_ref, scale_ref, partial2_ref, c2_ref):
    core = lax.axis_index("c")
    e = expander()
    scale = dot(factor_ref[...], e)
    cs = bc_ref[pl.ds(pl.multiple_of(T * core, T), T), pl.ds(2 * T, 2 * T)]
    for g in range(4):
        lanes = pl.ds(GW * g, GW)
        inter = dot(cs[:, N * g : N * g + N], entering(h_ref, g)) * scale[:, GW * g : GW * g + GW]
        out_ref[:, lanes] = (partial_ref[:, lanes] + inter).astype(BF16)
    c2_ref[...] = swap_ref[:, pl.ds(2 * HW, 2 * T)]
    scale_ref[...] = dot(swap_ref[:, pl.ds(2 * HW + 2 * T, T)], e)
    for g in range(4):
        lanes = pl.ds(GW * g, GW)
        low = swap_ref[:, pl.ds(HW + GW * g, GW)]
        partial2_ref[:, lanes] = swap_ref[:, lanes].astype(F32) + low.astype(F32)


def final_kernel(mine_ref, scale_ref, partial_ref, c_ref, h_ref, out_hbm, other_ref, sems):
    core = lax.axis_index("c")

    def copy(src, n, half):
        return pltpu.make_async_copy(src, out_hbm.at[:, pl.ds(HW * half, HW)], sems.at[n])

    for k in range(2):

        @pl.when(core == k)
        def _():
            copy(mine_ref, 0, k).start()

    cs = c_ref[...]
    for g in range(4):
        lanes = pl.ds(GW * g, GW)
        inter = dot(cs[:, N * g : N * g + N], entering(h_ref, g)) * scale_ref[:, lanes]
        partial = partial_ref[:, lanes]
        other_ref[:, lanes] = (partial + inter).astype(BF16)
    for k in range(2):

        @pl.when(core == k)
        def _():
            copy(other_ref, 1, 1 - k).start()
            copy(mine_ref, 0, k).wait()
            copy(other_ref, 1, 1 - k).wait()


def per_device(x, b, c, dt, order, resets, rate, skip):
    core = lax.axis_index("c")
    sds = jax.ShapeDtypeStruct
    hbm, vmem = pl.BlockSpec(memory_space=pltpu.HBM), pl.BlockSpec(memory_space=pltpu.VMEM)
    resets = resets.reshape(1, T)
    packed = pl.pallas_call(
        pack_kernel,
        out_shape=sds((2 * NX, NZ, MSG, T), BF16),
        in_specs=[hbm] * 5,
        out_specs=hbm,
        scratch_shapes=[
            pltpu.VMEM(x.shape, BF16),
            pltpu.VMEM(b.shape, BF16),
            pltpu.VMEM(c.shape, BF16),
            pltpu.VMEM(dt.shape[::-1], BF16),
            pltpu.VMEM((1, T), I32),
            pltpu.VMEM((2 * NX, NZ, MSG, T), BF16),
            pltpu.SemaphoreType.DMA((2 + 3 * PARTS,)),
            pltpu.SemaphoreType.DMA((PARTS,)),
        ],
        compiler_params=params(56),
        name="pack",
    )(x, b, c, dt.T, resets)
    packed = packed.reshape(2 * NP, MSG, T)
    arrived = lax.all_to_all(packed, ("x", "c", "z"), split_axis=0, concat_axis=0, tiled=True)
    order2 = lax.ppermute(order, "c", [(0, 1), (1, 0)])
    resets2 = lax.ppermute(resets, "c", [(0, 1), (1, 0)])
    perm, cnt = pl.pallas_call(
        plan_kernel,
        out_shape=(sds((2 * T, 2 * T), BF16), sds((T, T), F32)),
        compiler_params=params(16),
        cost_estimate=pl.CostEstimate(flops=1_000_000_000, bytes_accessed=1_000_000, transcendentals=0),
        name="plan",
    )(order, order2, resets, resets2)
    mine = lax.dynamic_slice_in_dim(rate, core * HH, HH)
    rate_row = jnp.concatenate([mine, mine, jnp.zeros((64,), F32)]).reshape(1, T)
    pair = (lax.axis_index("x") * NZ + lax.axis_index("z")) // 2 * 2
    pair_row = jnp.repeat(lax.dynamic_slice_in_dim(rate, core * HH + pair, 2), HP).reshape(1, T)
    skip_row = jnp.repeat(lax.dynamic_slice_in_dim(skip, core * HH, HH), HP).reshape(1, HW)
    xs, bc, cum, step, msg, sums = pl.pallas_call(
        state_kernel,
        out_shape=(
            sds((AWAY, HW), BF16),
            sds((2 * T, 4 * T), BF16),
            sds((T, T), F32),
            sds((T, T), F32),
            sds((NP, 32, T), BF16),
            sds((8, T), F32),
        ),
        out_specs=(hbm,) + (vmem,) * 3 + (hbm, vmem),
        scratch_shapes=[
            pltpu.VMEM((2 * T, HW), BF16),
            pltpu.SemaphoreType.DMA((4,)),
            pltpu.VMEM((NP, 32, T), BF16),
            pltpu.SemaphoreType.DMA((4,)),
        ],
        compiler_params=params(24),
        name="state",
    )(arrived, rate_row, perm, cnt)
    totals = lax.all_to_all(msg, ("x", "z"), split_axis=0, concat_axis=0, tiled=True)
    partial, factors, swap, decays = pl.pallas_call(
        local_kernel,
        out_shape=(sds((T, HW), F32), sds((T, T), BF16), sds((T, 2 * HW + 3 * T), BF16), sds((NP, T), F32)),
        in_specs=[hbm] + [vmem] * 7,
        scratch_shapes=[
            pltpu.VMEM((2 * T, HW), F32),
            pltpu.VMEM((T, T), F32),
            pltpu.VMEM((2 * T, HW), BF16),
            pltpu.SemaphoreType.DMA,
        ],
        compiler_params=params(20),
        cost_estimate=pl.CostEstimate(flops=2_000_000_000, bytes_accessed=6_000_000, transcendentals=1_100_000),
        name="local",
    )(xs, bc, cum, step, cnt, skip_row, sums, pair_row)
    swap = lax.ppermute(swap, "c", [(0, 1), (1, 0)])
    prefixes = pl.pallas_call(
        scan_kernel, out_shape=sds((NP, 32, T), BF16), compiler_params=params(16), name="chips"
    )(totals, decays)
    states = lax.all_to_all(prefixes, ("x", "z"), split_axis=0, concat_axis=0, tiled=True)
    other = lax.ppermute(states, "c", [(0, 1), (1, 0)])
    own, scale, partial2, c2 = pl.pallas_call(
        mine_kernel,
        out_shape=(sds((T, HW), BF16), sds((T, HW), F32), sds((T, HW), F32), sds((T, 2 * T), BF16)),
        compiler_params=params(20),
        name="mine",
    )(partial, bc, factors, states, swap)
    return pl.pallas_call(
        final_kernel,
        out_shape=sds((T, 2 * HW), BF16),
        in_specs=[vmem] * 5,
        out_specs=hbm,
        scratch_shapes=[pltpu.VMEM((T, HW), BF16), pltpu.SemaphoreType.DMA((2,))],
        compiler_params=params(20),
        name="final",
    )(own, scale, partial2, c2, other)


def solution(mesh):
    fine = Mesh(mesh.devices.reshape(NZ, NX, 2, mesh.shape["seq"]), ("z", "x", "c", "seq"))
    rows = ("seq", "z", "x", "c")
    in_specs = (P(rows, None),) * 5 + (P(rows), P(), P())
    return jax.shard_map(
        per_device, mesh=fine, in_specs=in_specs, out_specs=P(rows, None), check_vma=False
    )
```

```python
import jax
import jax.numpy as jnp
from jax import lax
from jax.experimental import pallas as pl
from jax.experimental.pallas import tpu as pltpu
from jax.sharding import Mesh, PartitionSpec as P

F32 = jnp.float32
BF16 = jnp.bfloat16
I32 = jnp.int32
T = 128
NX, NZ = 4, 8
NP = NX * NZ
HG = 8
HP = 64
N = 64
GW = HG * HP
HH = 32
HW = HH * HP
MSG = 88
PARTS = 2
AWAY = 12288


def iota(shape, dim):
    return lax.broadcasted_iota(I32, shape, dim)


def dot(a, b):
    return jnp.dot(a, b, preferred_element_type=F32)


def dot_nt(a, b):
    return lax.dot_general(a, b, (((1,), (1,)), ((), ())), preferred_element_type=F32)


def params(mib):
    return pltpu.CompilerParams(vmem_limit_bytes=mib * 1024 * 1024)


def softplus(v):
    return jnp.maximum(v, 0.0) + jnp.log1p(jnp.exp(-jnp.abs(v)))


def three_parts(v):
    high = v.astype(BF16)
    rest = v - high.astype(F32)
    mid = rest.astype(BF16)
    return high, mid, (rest - mid.astype(F32)).astype(BF16)


def pack_kernel(
    x_hbm, b_hbm, c_hbm, dt_hbm, reset_hbm, out_hbm,
    x_ref, b_ref, c_ref, dt_ref, reset_ref, out_ref, sems, out_sems,
):
    pairs = [(reset_hbm, reset_ref), (dt_hbm, dt_ref)]
    span = T // PARTS
    for part in range(PARTS):
        rows = pl.ds(span * part, span)
        pairs += [(src.at[rows], dst.at[rows]) for src, dst in ((b_hbm, b_ref), (c_hbm, c_ref), (x_hbm, x_ref))]
    copies = [pltpu.make_async_copy(s, d, sems.at[n]) for n, (s, d) in enumerate(pairs)]
    for copy in copies:
        copy.start()
    row, col = iota((4 * span, 4 * span), 0), iota((4 * span, 4 * span), 1)
    pick = (col // span == (row % 16) // 4) & (col % span == (row // 16) * 4 + row % 4)
    pick = pick.astype(BF16)
    lane, head = iota((256, 64), 0), iota((256, 64), 1)
    spread = (lane % T < HH) & (head == (lane // T) * HH + lane % T)
    to, row = iota((256, T), 0), iota((256, T), 1)
    own_row = ((to % 8 < 4) & (row == (to // 8) * 4 + to % 8)).astype(BF16)
    to, head = iota((256, 64), 0), iota((256, 64), 1)
    chosen = ((to % 8 // 2 == 2) & (head == 2 * (to // 8) + to % 2)).astype(BF16)
    of_chip = (iota((T, T), 0) // 4 == iota((T, T), 1)).astype(BF16)
    chip = lax.axis_index("z") * NX + lax.axis_index("x")
    flag = (iota((8, T), 0) == 6) & (iota((8, T), 1) == chip)
    for copy in copies[:2]:
        copy.wait()
    dt = dt_ref[...]
    wide = dot(spread.astype(BF16), dt).astype(BF16)
    steps = dot_nt(own_row, wide)
    sums = dot(jnp.concatenate(three_parts(softplus(dt.astype(F32))), axis=0), of_chip)
    high, mid, low = three_parts(sums[:64] + sums[64:128] + sums[128:])
    sums = high.astype(F32) + pltpu.roll(mid.astype(F32), HH, 1) + pltpu.roll(low.astype(F32), 2 * HH, 1)
    sums = dot(chosen, sums.astype(BF16))
    resets = jnp.sum(reset_ref[...].astype(F32), axis=1, keepdims=True)
    flag = jnp.where(flag, jnp.broadcast_to(resets, (8, T)), 0.0)
    sent = []
    for part in range(PARTS):
        for copy in copies[2 + 3 * part : 5 + 3 * part]:
            copy.wait()
        rows = pl.ds(span * part, span)
        tiles = []
        for c in range(2):
            for q in range(4):
                tiles.append([x_ref[rows, pl.ds(HW * c + 512 * q + T * j, T)] for j in range(4)])
            tiles.append(
                [b_ref[rows, pl.ds(256 * c, T)], b_ref[rows, pl.ds(256 * c + T, T)],
                 c_ref[rows, pl.ds(256 * c, T)], c_ref[rows, pl.ds(256 * c + T, T)]]
            )
        right = jnp.concatenate([jnp.concatenate(t, axis=0) for t in tiles], axis=1)
        got = dot(pick, right).astype(BF16)
        for p in range(NP // PARTS):
            z, x = NZ // PARTS * part + p // NX, p % NX
            at = 8 * (NP // PARTS * part + p)
            for c in range(2):
                to = 2 * x + c
                for q in range(5):
                    lanes = slice(T * (5 * c + q), T * (5 * c + q) + T)
                    out_ref[z, to, pl.ds(16 * q, 16), :] = got[16 * p : 16 * p + 16, lanes]
                m = 8 * (16 * c + (NZ * x + z) // 2)
                tail = steps[at : at + 8, T * c : T * c + T] + sums[m : m + 8] + flag
                out_ref[z, to, pl.ds(80, 8), :] = tail.astype(BF16)
        here = pl.ds(NZ // PARTS * part, NZ // PARTS)
        sent.append(pltpu.make_async_copy(out_ref.at[here], out_hbm.at[here], out_sems.at[part]))
        sent[-1].start()
    for copy in sent:
        copy.wait()


def columns(row):
    return jnp.broadcast_to(row, (T, T)).T


def plan_kernel(order_ref, order2_ref, reset_ref, reset2_ref, perm_ref, cnt_ref):
    core = lax.axis_index("c")
    orders = [order_ref[...].astype(F32), order2_ref[...].astype(F32)]
    resets = [reset_ref[...].astype(F32), reset2_ref[...].astype(F32)]
    orders = [columns(jnp.where(core == i, orders[0], orders[1])) for i in range(2)]
    upto = (iota((T, T), 0) <= iota((T, T), 1)).astype(BF16)
    counts = []
    for i in range(2):
        row = jnp.broadcast_to(jnp.where(core == i, resets[0], resets[1]), (8, T))
        counts.append(columns(dot(row.astype(BF16), upto)[:1]))
    cnt_ref[...] = jnp.where(iota((T, T), 1) < HH, counts[0], counts[1])
    order = jnp.concatenate(orders, axis=0).astype(I32)
    source = order >> 1
    target = (source << 2) + ((iota((256, T), 0) >> 7) << 1) + (order & 1)
    for m in range(2):
        perm_ref[:, pl.ds(T * m, T)] = jnp.where(iota((256, T), 1) + T * m == target, 1.0, 0.0).astype(BF16)


def expander():
    gap = iota((T, T), 0) % HH - iota((T, T), 1) // HP
    return jnp.concatenate([jnp.where(gap == 2 * t, 1.0, 0.0).astype(BF16) for t in range(HW // T)], axis=1)


def two_parts(v):
    high = v.astype(BF16).astype(F32)
    low = v - high
    return jnp.where(iota(v.shape, 1) < 64, high, pltpu.roll(low, 64, 1))


def of_span(parts, i):
    return jnp.where((iota(parts.shape, 1) % 64) // HH == i, parts, 0.0).astype(BF16)


def inner_weights(cum, step, cnt):
    last, last_cnt = cum[T - 1 : T], cnt[T - 1 : T]
    return two_parts(jnp.where(cnt == last_cnt, jnp.exp(last - cum) * step, 0.0))


def span_decay(cum, cnt):
    return jnp.where(cnt[T - 1 : T] == 0.0, jnp.exp(cum[T - 1 : T]), 0.0)


def x_tile(x_ref, rows, t):
    return x_ref[rows, pl.ds(T * (4 * (t % 4) + t // 4), T)]


def state_kernel(
    arrived_ref, rate_ref, perm_ref, cnt_ref, x_hbm, bc_ref, cum_ref, step_ref, msg_hbm, sums_ref, x_ref, x_sems, msg_ref, msg_sems
):
    top = iota((NP, 8, T), 1) < 4

    def halves(here):
        even, odd = here[:, 0], here[:, 1]
        low = jnp.where(top, even, pltpu.roll(odd, 4, 1)).reshape(256, T).astype(BF16)
        high = jnp.where(top, pltpu.roll(even, 4, 1), odd).reshape(256, T).astype(BF16)
        return low, high

    perm = perm_ref[...]
    cnt = cnt_ref[...]
    tails = arrived_ref[:, pl.ds(80, 8), :].astype(F32)
    sums_ref[...] = jnp.sum(tails, axis=0)
    raw = dot(perm, halves(tails.reshape(NP, 2, 8, T))[0])
    raw = jnp.where(iota((T, T), 1) < HH, raw[:T], pltpu.roll(raw[T:], HH, 1))
    step = softplus(raw)
    lower = (iota((T, T), 0) >= iota((T, T), 1)).astype(BF16)
    cum = dot(lower, jnp.concatenate(three_parts(-step * rate_ref[...]), axis=1))
    cum = cum[:, :T] + cum[:, T : 2 * T] + cum[:, 2 * T :]
    cum_ref[...] = cum
    step_ref[...] = step
    tiles = [[] for _ in range(4)]
    for q in range(5):
        here = arrived_ref[:, pl.ds(16 * q, 16), :].astype(F32).reshape(NP, 2, 2, 8, T)
        for half in range(2):
            low, high = halves(here[:, :, half])
            tiles[2 * half].append(low)
            tiles[2 * half + 1].append(high)
    x_copies = []
    for j in range(4):
        rows = dot(perm, jnp.concatenate(tiles[j], axis=1)).astype(BF16)
        here = pl.ds(GW * j, GW)
        x_ref[:, here] = rows[:, :GW]
        bc_ref[:, pl.ds(T * j, T)] = rows[:, GW:]
        x_copies.append(pltpu.make_async_copy(x_ref.at[:, here], x_hbm.at[pl.ds(0, 2 * T), here], x_sems.at[j]))
        x_copies[-1].start()
    e = expander()
    coef = inner_weights(cum, step, cnt)
    decay = two_parts(jnp.broadcast_to(span_decay(cum, cnt), (8, T)))
    decay = dot(of_span(decay, 1), e)[:1]
    weighted = []
    for i in range(2):
        here = pl.ds(T * i, T)
        scale = dot(of_span(coef, i), e)
        weighted.append([(x_tile(x_ref, here, t).astype(F32) * scale[:, T * t : T * t + T]).astype(BF16) for t in range(16)])
    for tile in range(2):
        b = [bc_ref[pl.ds(T * i, T), pl.ds(T * tile, T)].astype(F32).T.astype(BF16) for i in range(2)]
        for half in range(2):
            g = 2 * tile + half
            lanes = slice(GW * g, GW * g + GW)
            states = [dot(b[i][N * half : N * half + N], jnp.concatenate(weighted[i][4 * g : 4 * g + 4], axis=1)) for i in range(2)]
            h = (decay[:, lanes] * states[0] + states[1]).astype(BF16)
            for pair in range(4):
                for k in range(2):
                    m = (4 * g + pair) * 2 + k
                    msg_ref[m] = h[32 * k : 32 * k + 32, T * pair : T * pair + T]
            part = pl.ds(8 * g, 8)
            x_copies.append(pltpu.make_async_copy(msg_ref.at[part], msg_hbm.at[part], msg_sems.at[g]))
            x_copies[-1].start()
    for copy in x_copies:
        copy.wait()


def local_kernel(
    x_hbm, bc_ref, cum_ref, step_ref, cnt_ref, skip_ref, sums_ref, pair_ref,
    mine_ref, factor_ref, swap_ref, decay_ref, out_ref, key_ref, x_ref, x_sem,
):
    x_copy = pltpu.make_async_copy(x_hbm.at[pl.ds(0, 2 * T)], x_ref, x_sem)
    x_copy.start()
    core = lax.axis_index("c")
    there = pl.ds(pl.multiple_of(T * (1 - core), T), T)
    cum, step, cnt = cum_ref[...], step_ref[...], cnt_ref[...]
    key_ref[...] = (cum - jnp.log(step)).T
    entry = jnp.where(cnt == 0.0, jnp.exp(cum), 0.0)
    decay = jnp.broadcast_to(span_decay(cum, cnt), (8, T))
    before = jnp.where(iota((8, T), 1) < HH, 1.0, pltpu.roll(decay, HH, 1))
    carry = two_parts(entry * before[:1])
    factor_ref[...] = of_span(carry, core)
    e = expander()
    entry = dot(of_span(two_parts(entry), 1), e)
    causal = iota((T, T), 0) >= iota((T, T), 1)
    keeps, scores = [], []
    for i in range(2):
        here = pl.ds(T * i, T)
        count = jnp.broadcast_to(cnt[:, HH * i : HH * i + 1], (T, T))
        keeps.append(causal & (count == count.T))
        for g in range(4):
            lanes = slice(N * (g % 2), N * (g % 2) + N)
            b = bc_ref[here, pl.ds(T * (g // 2), T)][:, lanes]
            c = bc_ref[here, pl.ds(2 * T + T * (g // 2), T)][:, lanes]
            scores.append(dot_nt(c, b))
    x_copy.wait()
    inner = dot(of_span(inner_weights(cum, step, cnt), 0), e)
    weighted = [
        (x_tile(x_ref, pl.ds(0, T), t).astype(F32) * inner[:, T * t : T * t + T]).astype(BF16) for t in range(16)
    ]
    left = iota((T, T), 1) < HP
    for i in range(2):
        here = pl.ds(T * i, T)
        for g in range(4):
            tile, half = g // 2, g % 2
            if i == 1:
                c = bc_ref[here, pl.ds(2 * T + T * tile, T)][:, N * half : N * half + N]
                lanes = slice(GW * g, GW * g + GW)
                first = bc_ref[pl.ds(0, T), pl.ds(T * tile, T)].astype(F32).T[N * half : N * half + N].astype(BF16)
                state = dot(first, jnp.concatenate(weighted[4 * g : 4 * g + 4], axis=1)).astype(BF16)
                carried = dot(c, state) * entry[:, lanes]
            for pair in range(4):
                weights = []
                for h in (2 * pair, 2 * pair + 1):
                    col = HH * i + HG * g + h
                    gap = cum_ref[:, col : col + 1] - key_ref[col : col + 1, :]
                    weights.append((jnp.exp(jnp.where(keeps[i], gap, -jnp.inf)) * scores[4 * i + g]).astype(BF16))
                lanes = pl.ds(GW * g + T * pair, T)
                x = x_tile(x_ref, here, 4 * g + pair)
                zero = jnp.zeros_like(x)
                both = jnp.concatenate([jnp.where(left, x, zero), jnp.where(left, zero, x)], axis=0)
                out = dot(jnp.concatenate(weights, axis=1), both) + skip_ref[:, lanes] * x.astype(F32)
                if i == 1:
                    out += carried[:, T * pair : T * pair + T]
                out_ref[here, lanes] = out
    mine_ref[...] = out_ref[pl.ds(pl.multiple_of(T * core, T), T), :]
    other = out_ref[there, :]
    high = other.astype(BF16)
    swap_ref[:, pl.ds(0, HW)] = high
    swap_ref[:, pl.ds(HW, HW)] = (other - high.astype(F32)).astype(BF16)
    swap_ref[:, pl.ds(2 * HW, 2 * T)] = bc_ref[there, pl.ds(2 * T, 2 * T)]
    swap_ref[:, pl.ds(2 * HW + 2 * T, T)] = of_span(carry, 1 - core)
    tails = sums_ref[...]
    sums = tails + pltpu.roll(tails, T - HH, 1) + pltpu.roll(tails, T - 2 * HH, 1)
    rows = iota((8, T), 0)
    sums = jnp.where(rows == 6, tails, sums)
    sums = jnp.concatenate([sums, jnp.zeros((T - 8, T), F32)], axis=0).T[:NP]
    resets = sums[:, 6:7]
    sums = jnp.where(iota((NP, T), 1) < HP, sums[:, 4:5], sums[:, 5:6])
    decay_ref[...] = jnp.where(resets == 0.0, jnp.exp(-sums * pair_ref[...]), 0.0)


def scan_kernel(in_ref, decay_ref, out_ref):
    h = jnp.zeros((32, T), F32)
    for p in range(NP):
        at = (p % NX) * NZ + p // NX
        out_ref[at] = h.astype(BF16)
        h = decay_ref[pl.ds(p, 1), :] * h + in_ref[at].astype(F32)


def entering(h_ref, g):
    return jnp.concatenate(
        [jnp.concatenate([h_ref[8 * g + 2 * p], h_ref[8 * g + 2 * p + 1]], axis=0) for p in range(4)], axis=1
    )


def mine_kernel(partial_ref, bc_ref, factor_ref, h_ref, swap_ref, out_ref, scale_ref, partial2_ref, c2_ref):
    core = lax.axis_index("c")
    e = expander()
    scale = dot(factor_ref[...], e)
    cs = bc_ref[pl.ds(pl.multiple_of(T * core, T), T), pl.ds(2 * T, 2 * T)]
    for g in range(4):
        lanes = pl.ds(GW * g, GW)
        inter = dot(cs[:, N * g : N * g + N], entering(h_ref, g)) * scale[:, GW * g : GW * g + GW]
        out_ref[:, lanes] = (partial_ref[:, lanes] + inter).astype(BF16)
    c2_ref[...] = swap_ref[:, pl.ds(2 * HW, 2 * T)]
    scale_ref[...] = dot(swap_ref[:, pl.ds(2 * HW + 2 * T, T)], e)
    for g in range(4):
        lanes = pl.ds(GW * g, GW)
        low = swap_ref[:, pl.ds(HW + GW * g, GW)]
        partial2_ref[:, lanes] = swap_ref[:, lanes].astype(F32) + low.astype(F32)


def final_kernel(mine_ref, scale_ref, partial_ref, c_ref, h_ref, out_hbm, other_ref, sems):
    core = lax.axis_index("c")

    def copy(src, n, half):
        return pltpu.make_async_copy(src, out_hbm.at[:, pl.ds(HW * half, HW)], sems.at[n])

    for k in range(2):

        @pl.when(core == k)
        def _():
            copy(mine_ref, 0, k).start()

    cs = c_ref[...]
    for g in range(4):
        lanes = pl.ds(GW * g, GW)
        inter = dot(cs[:, N * g : N * g + N], entering(h_ref, g)) * scale_ref[:, lanes]
        partial = partial_ref[:, lanes]
        other_ref[:, lanes] = (partial + inter).astype(BF16)
    for k in range(2):

        @pl.when(core == k)
        def _():
            copy(other_ref, 1, 1 - k).start()
            copy(mine_ref, 0, k).wait()
            copy(other_ref, 1, 1 - k).wait()


def per_device(x, b, c, dt, order, resets, rate, skip):
    core = lax.axis_index("c")
    sds = jax.ShapeDtypeStruct
    hbm, vmem = pl.BlockSpec(memory_space=pltpu.HBM), pl.BlockSpec(memory_space=pltpu.VMEM)
    resets = resets.reshape(1, T)
    packed = pl.pallas_call(
        pack_kernel,
        out_shape=sds((NZ, 2 * NX, MSG, T), BF16),
        in_specs=[hbm] * 5,
        out_specs=hbm,
        scratch_shapes=[
            pltpu.VMEM(x.shape, BF16),
            pltpu.VMEM(b.shape, BF16),
            pltpu.VMEM(c.shape, BF16),
            pltpu.VMEM(dt.shape[::-1], BF16),
            pltpu.VMEM((1, T), I32),
            pltpu.VMEM((NZ, 2 * NX, MSG, T), BF16),
            pltpu.SemaphoreType.DMA((2 + 3 * PARTS,)),
            pltpu.SemaphoreType.DMA((PARTS,)),
        ],
        compiler_params=params(56),
        name="pack",
    )(x, b, c, dt.T, resets)
    packed = packed.reshape(2 * NP, MSG, T)
    arrived = lax.all_to_all(packed, ("z", "x", "c"), split_axis=0, concat_axis=0, tiled=True)
    order2 = lax.ppermute(order, "c", [(0, 1), (1, 0)])
    resets2 = lax.ppermute(resets, "c", [(0, 1), (1, 0)])
    perm, cnt = pl.pallas_call(
        plan_kernel,
        out_shape=(sds((2 * T, 2 * T), BF16), sds((T, T), F32)),
        compiler_params=params(16),
        cost_estimate=pl.CostEstimate(flops=1_000_000_000, bytes_accessed=1_000_000, transcendentals=0),
        name="plan",
    )(order, order2, resets, resets2)
    mine = lax.dynamic_slice_in_dim(rate, core * HH, HH)
    rate_row = jnp.concatenate([mine, mine, jnp.zeros((64,), F32)]).reshape(1, T)
    pair = (lax.axis_index("x") * NZ + lax.axis_index("z")) // 2 * 2
    pair_row = jnp.repeat(lax.dynamic_slice_in_dim(rate, core * HH + pair, 2), HP).reshape(1, T)
    skip_row = jnp.repeat(lax.dynamic_slice_in_dim(skip, core * HH, HH), HP).reshape(1, HW)
    xs, bc, cum, step, msg, sums = pl.pallas_call(
        state_kernel,
        out_shape=(
            sds((AWAY, HW), BF16),
            sds((2 * T, 4 * T), BF16),
            sds((T, T), F32),
            sds((T, T), F32),
            sds((NP, 32, T), BF16),
            sds((8, T), F32),
        ),
        out_specs=(hbm,) + (vmem,) * 3 + (hbm, vmem),
        scratch_shapes=[
            pltpu.VMEM((2 * T, HW), BF16),
            pltpu.SemaphoreType.DMA((4,)),
            pltpu.VMEM((NP, 32, T), BF16),
            pltpu.SemaphoreType.DMA((4,)),
        ],
        compiler_params=params(24),
        name="state",
    )(arrived, rate_row, perm, cnt)
    totals = lax.all_to_all(msg, ("x", "z"), split_axis=0, concat_axis=0, tiled=True)
    partial, factors, swap, decays = pl.pallas_call(
        local_kernel,
        out_shape=(sds((T, HW), F32), sds((T, T), BF16), sds((T, 2 * HW + 3 * T), BF16), sds((NP, T), F32)),
        in_specs=[hbm] + [vmem] * 7,
        scratch_shapes=[
            pltpu.VMEM((2 * T, HW), F32),
            pltpu.VMEM((T, T), F32),
            pltpu.VMEM((2 * T, HW), BF16),
            pltpu.SemaphoreType.DMA,
        ],
        compiler_params=params(20),
        cost_estimate=pl.CostEstimate(flops=2_000_000_000, bytes_accessed=6_000_000, transcendentals=1_100_000),
        name="local",
    )(xs, bc, cum, step, cnt, skip_row, sums, pair_row)
    swap = lax.ppermute(swap, "c", [(0, 1), (1, 0)])
    prefixes = pl.pallas_call(
        scan_kernel, out_shape=sds((NP, 32, T), BF16), compiler_params=params(16), name="chips"
    )(totals, decays)
    states = lax.all_to_all(prefixes, ("x", "z"), split_axis=0, concat_axis=0, tiled=True)
    other = lax.ppermute(states, "c", [(0, 1), (1, 0)])
    own, scale, partial2, c2 = pl.pallas_call(
        mine_kernel,
        out_shape=(sds((T, HW), BF16), sds((T, HW), F32), sds((T, HW), F32), sds((T, 2 * T), BF16)),
        compiler_params=params(20),
        name="mine",
    )(partial, bc, factors, states, swap)
    return pl.pallas_call(
        final_kernel,
        out_shape=sds((T, 2 * HW), BF16),
        in_specs=[vmem] * 5,
        out_specs=hbm,
        scratch_shapes=[pltpu.VMEM((T, HW), BF16), pltpu.SemaphoreType.DMA((2,))],
        compiler_params=params(20),
        name="final",
    )(own, scale, partial2, c2, other)


def solution(mesh):
    fine = Mesh(mesh.devices.reshape(NZ, NX, 2, mesh.shape["seq"]), ("z", "x", "c", "seq"))
    rows = ("seq", "z", "x", "c")
    in_specs = (P(rows, None),) * 5 + (P(rows), P(), P())
    return jax.shard_map(
        per_device, mesh=fine, in_specs=in_specs, out_specs=P(rows, None), check_vma=False
    )
```

```python
import jax
import jax.numpy as jnp
from jax import lax
from jax.experimental import pallas as pl
from jax.experimental.pallas import tpu as pltpu
from jax.sharding import Mesh, PartitionSpec as P

F32 = jnp.float32
BF16 = jnp.bfloat16
I32 = jnp.int32
T = 128
NX, NZ = 4, 8
NP = NX * NZ
HG = 8
HP = 64
N = 64
GW = HG * HP
HH = 32
HW = HH * HP
MSG = 88
PARTS = (64, 48, 16)
AWAY = 12288


def iota(shape, dim):
    return lax.broadcasted_iota(I32, shape, dim)


def dot(a, b):
    return jnp.dot(a, b, preferred_element_type=F32)


def dot_nt(a, b):
    return lax.dot_general(a, b, (((1,), (1,)), ((), ())), preferred_element_type=F32)


def params(mib):
    return pltpu.CompilerParams(vmem_limit_bytes=mib * 1024 * 1024)


def softplus(v):
    return jnp.maximum(v, 0.0) + jnp.log1p(jnp.exp(-jnp.abs(v)))


def three_parts(v):
    high = v.astype(BF16)
    rest = v - high.astype(F32)
    mid = rest.astype(BF16)
    return high, mid, (rest - mid.astype(F32)).astype(BF16)


def pack_kernel(
    x_hbm, b_hbm, c_hbm, dt_hbm, reset_hbm, out_hbm,
    x_ref, b_ref, c_ref, dt_ref, reset_ref, out_ref, sems, out_sems,
):
    pairs = [(reset_hbm, reset_ref), (dt_hbm, dt_ref)]
    for part, span in enumerate(PARTS):
        rows = pl.ds(sum(PARTS[:part]), span)
        pairs += [(src.at[rows], dst.at[rows]) for src, dst in ((b_hbm, b_ref), (c_hbm, c_ref), (x_hbm, x_ref))]
    copies = [pltpu.make_async_copy(s, d, sems.at[n]) for n, (s, d) in enumerate(pairs)]
    for copy in copies:
        copy.start()
    picks = []
    for span in PARTS:
        row, col = iota((4 * span, 4 * span), 0), iota((4 * span, 4 * span), 1)
        pick = (col // span == (row % 16) // 4) & (col % span == (row // 16) * 4 + row % 4)
        picks.append(pick.astype(BF16))
    lane, head = iota((256, 64), 0), iota((256, 64), 1)
    spread = (lane % T < HH) & (head == (lane // T) * HH + lane % T)
    to, row = iota((256, T), 0), iota((256, T), 1)
    own_row = ((to % 8 < 4) & (row == (to // 8) * 4 + to % 8)).astype(BF16)
    to, head = iota((256, 64), 0), iota((256, 64), 1)
    chosen = ((to % 8 // 2 == 2) & (head == 2 * (to // 8) + to % 2)).astype(BF16)
    of_chip = (iota((T, T), 0) // 4 == iota((T, T), 1)).astype(BF16)
    chip = lax.axis_index("z") * NX + lax.axis_index("x")
    flag = (iota((8, T), 0) == 6) & (iota((8, T), 1) == chip)
    for copy in copies[:2]:
        copy.wait()
    dt = dt_ref[...]
    wide = dot(spread.astype(BF16), dt).astype(BF16)
    steps = dot_nt(own_row, wide)
    sums = dot(jnp.concatenate(three_parts(softplus(dt.astype(F32))), axis=0), of_chip)
    high, mid, low = three_parts(sums[:64] + sums[64:128] + sums[128:])
    sums = high.astype(F32) + pltpu.roll(mid.astype(F32), HH, 1) + pltpu.roll(low.astype(F32), 2 * HH, 1)
    sums = dot(chosen, sums.astype(BF16))
    resets = jnp.sum(reset_ref[...].astype(F32), axis=1, keepdims=True)
    flag = jnp.where(flag, jnp.broadcast_to(resets, (8, T)), 0.0)
    sent = []
    for part, span in enumerate(PARTS):
        for copy in copies[2 + 3 * part : 5 + 3 * part]:
            copy.wait()
        start = sum(PARTS[:part])
        rows = pl.ds(start, span)
        tiles = []
        for c in range(2):
            for q in range(4):
                tiles.append([x_ref[rows, pl.ds(HW * c + 512 * q + T * j, T)] for j in range(4)])
            tiles.append(
                [b_ref[rows, pl.ds(256 * c, T)], b_ref[rows, pl.ds(256 * c + T, T)],
                 c_ref[rows, pl.ds(256 * c, T)], c_ref[rows, pl.ds(256 * c + T, T)]]
            )
        right = jnp.concatenate([jnp.concatenate(t, axis=0) for t in tiles], axis=1)
        got = dot(picks[part], right).astype(BF16)
        for p in range(span // 4):
            z, x = start // 16 + p // NX, p % NX
            at = 8 * (start // 4 + p)
            for c in range(2):
                to = 2 * x + c
                for q in range(5):
                    lanes = slice(T * (5 * c + q), T * (5 * c + q) + T)
                    out_ref[z, to, pl.ds(16 * q, 16), :] = got[16 * p : 16 * p + 16, lanes]
                m = 8 * (16 * c + (NZ * x + z) // 2)
                tail = steps[at : at + 8, T * c : T * c + T] + sums[m : m + 8] + flag
                out_ref[z, to, pl.ds(80, 8), :] = tail.astype(BF16)
        here = pl.ds(start // 16, span // 16)
        sent.append(pltpu.make_async_copy(out_ref.at[here], out_hbm.at[here], out_sems.at[part]))
        sent[-1].start()
    for copy in sent:
        copy.wait()


def columns(row):
    return jnp.broadcast_to(row, (T, T)).T


def plan_kernel(order_ref, order2_ref, reset_ref, reset2_ref, perm_ref, cnt_ref):
    core = lax.axis_index("c")
    orders = [order_ref[...].astype(F32), order2_ref[...].astype(F32)]
    resets = [reset_ref[...].astype(F32), reset2_ref[...].astype(F32)]
    orders = [columns(jnp.where(core == i, orders[0], orders[1])) for i in range(2)]
    upto = (iota((T, T), 0) <= iota((T, T), 1)).astype(BF16)
    counts = []
    for i in range(2):
        row = jnp.broadcast_to(jnp.where(core == i, resets[0], resets[1]), (8, T))
        counts.append(columns(dot(row.astype(BF16), upto)[:1]))
    cnt_ref[...] = jnp.where(iota((T, T), 1) < HH, counts[0], counts[1])
    order = jnp.concatenate(orders, axis=0).astype(I32)
    source = order >> 1
    target = (source << 2) + ((iota((256, T), 0) >> 7) << 1) + (order & 1)
    for m in range(2):
        perm_ref[:, pl.ds(T * m, T)] = jnp.where(iota((256, T), 1) + T * m == target, 1.0, 0.0).astype(BF16)


def expander():
    gap = iota((T, T), 0) % HH - iota((T, T), 1) // HP
    return jnp.concatenate([jnp.where(gap == 2 * t, 1.0, 0.0).astype(BF16) for t in range(HW // T)], axis=1)


def two_parts(v):
    high = v.astype(BF16).astype(F32)
    low = v - high
    return jnp.where(iota(v.shape, 1) < 64, high, pltpu.roll(low, 64, 1))


def of_span(parts, i):
    return jnp.where((iota(parts.shape, 1) % 64) // HH == i, parts, 0.0).astype(BF16)


def inner_weights(cum, step, cnt):
    last, last_cnt = cum[T - 1 : T], cnt[T - 1 : T]
    return two_parts(jnp.where(cnt == last_cnt, jnp.exp(last - cum) * step, 0.0))


def span_decay(cum, cnt):
    return jnp.where(cnt[T - 1 : T] == 0.0, jnp.exp(cum[T - 1 : T]), 0.0)


def x_tile(x_ref, rows, t):
    return x_ref[rows, pl.ds(T * (4 * (t % 4) + t // 4), T)]


def state_kernel(
    arrived_ref, rate_ref, perm_ref, cnt_ref, x_hbm, bc_ref, cum_ref, step_ref, msg_hbm, sums_ref, x_ref, x_sems, msg_ref, msg_sems
):
    top = iota((NP, 8, T), 1) < 4

    def halves(here):
        even, odd = here[:, 0], here[:, 1]
        low = jnp.where(top, even, pltpu.roll(odd, 4, 1)).reshape(256, T).astype(BF16)
        high = jnp.where(top, pltpu.roll(even, 4, 1), odd).reshape(256, T).astype(BF16)
        return low, high

    perm = perm_ref[...]
    cnt = cnt_ref[...]
    tails = arrived_ref[:, pl.ds(80, 8), :].astype(F32)
    sums_ref[...] = jnp.sum(tails, axis=0)
    raw = dot(perm, halves(tails.reshape(NP, 2, 8, T))[0])
    raw = jnp.where(iota((T, T), 1) < HH, raw[:T], pltpu.roll(raw[T:], HH, 1))
    step = softplus(raw)
    lower = (iota((T, T), 0) >= iota((T, T), 1)).astype(BF16)
    cum = dot(lower, jnp.concatenate(three_parts(-step * rate_ref[...]), axis=1))
    cum = cum[:, :T] + cum[:, T : 2 * T] + cum[:, 2 * T :]
    cum_ref[...] = cum
    step_ref[...] = step
    tiles = [[] for _ in range(4)]
    for q in range(5):
        here = arrived_ref[:, pl.ds(16 * q, 16), :].astype(F32).reshape(NP, 2, 2, 8, T)
        for half in range(2):
            low, high = halves(here[:, :, half])
            tiles[2 * half].append(low)
            tiles[2 * half + 1].append(high)
    x_copies = []
    for j in range(4):
        rows = dot(perm, jnp.concatenate(tiles[j], axis=1)).astype(BF16)
        here = pl.ds(GW * j, GW)
        x_ref[:, here] = rows[:, :GW]
        bc_ref[:, pl.ds(T * j, T)] = rows[:, GW:]
        x_copies.append(pltpu.make_async_copy(x_ref.at[:, here], x_hbm.at[pl.ds(0, 2 * T), here], x_sems.at[j]))
        x_copies[-1].start()
    e = expander()
    coef = inner_weights(cum, step, cnt)
    decay = two_parts(jnp.broadcast_to(span_decay(cum, cnt), (8, T)))
    decay = dot(of_span(decay, 1), e)[:1]
    weighted = []
    for i in range(2):
        here = pl.ds(T * i, T)
        scale = dot(of_span(coef, i), e)
        weighted.append([(x_tile(x_ref, here, t).astype(F32) * scale[:, T * t : T * t + T]).astype(BF16) for t in range(16)])
    for tile in range(2):
        b = [bc_ref[pl.ds(T * i, T), pl.ds(T * tile, T)].astype(F32).T.astype(BF16) for i in range(2)]
        for half in range(2):
            g = 2 * tile + half
            lanes = slice(GW * g, GW * g + GW)
            states = [dot(b[i][N * half : N * half + N], jnp.concatenate(weighted[i][4 * g : 4 * g + 4], axis=1)) for i in range(2)]
            h = (decay[:, lanes] * states[0] + states[1]).astype(BF16)
            for pair in range(4):
                for k in range(2):
                    m = (4 * g + pair) * 2 + k
                    msg_ref[m] = h[32 * k : 32 * k + 32, T * pair : T * pair + T]
            part = pl.ds(8 * g, 8)
            x_copies.append(pltpu.make_async_copy(msg_ref.at[part], msg_hbm.at[part], msg_sems.at[g]))
            x_copies[-1].start()
    for copy in x_copies:
        copy.wait()


def local_kernel(
    x_hbm, bc_ref, cum_ref, step_ref, cnt_ref, skip_ref, sums_ref, pair_ref,
    mine_ref, factor_ref, swap_ref, decay_ref, out_ref, key_ref, x_ref, x_sem,
):
    x_copy = pltpu.make_async_copy(x_hbm.at[pl.ds(0, 2 * T)], x_ref, x_sem)
    x_copy.start()
    core = lax.axis_index("c")
    there = pl.ds(pl.multiple_of(T * (1 - core), T), T)
    cum, step, cnt = cum_ref[...], step_ref[...], cnt_ref[...]
    key_ref[...] = (cum - jnp.log(step)).T
    entry = jnp.where(cnt == 0.0, jnp.exp(cum), 0.0)
    decay = jnp.broadcast_to(span_decay(cum, cnt), (8, T))
    before = jnp.where(iota((8, T), 1) < HH, 1.0, pltpu.roll(decay, HH, 1))
    carry = two_parts(entry * before[:1])
    factor_ref[...] = of_span(carry, core)
    e = expander()
    entry = dot(of_span(two_parts(entry), 1), e)
    causal = iota((T, T), 0) >= iota((T, T), 1)
    keeps, scores = [], []
    for i in range(2):
        here = pl.ds(T * i, T)
        count = jnp.broadcast_to(cnt[:, HH * i : HH * i + 1], (T, T))
        keeps.append(causal & (count == count.T))
        for g in range(4):
            lanes = slice(N * (g % 2), N * (g % 2) + N)
            b = bc_ref[here, pl.ds(T * (g // 2), T)][:, lanes]
            c = bc_ref[here, pl.ds(2 * T + T * (g // 2), T)][:, lanes]
            scores.append(dot_nt(c, b))
    x_copy.wait()
    inner = dot(of_span(inner_weights(cum, step, cnt), 0), e)
    weighted = [
        (x_tile(x_ref, pl.ds(0, T), t).astype(F32) * inner[:, T * t : T * t + T]).astype(BF16) for t in range(16)
    ]
    left = iota((T, T), 1) < HP
    for i in range(2):
        here = pl.ds(T * i, T)
        for g in range(4):
            tile, half = g // 2, g % 2
            if i == 1:
                c = bc_ref[here, pl.ds(2 * T + T * tile, T)][:, N * half : N * half + N]
                lanes = slice(GW * g, GW * g + GW)
                first = bc_ref[pl.ds(0, T), pl.ds(T * tile, T)].astype(F32).T[N * half : N * half + N].astype(BF16)
                state = dot(first, jnp.concatenate(weighted[4 * g : 4 * g + 4], axis=1)).astype(BF16)
                carried = dot(c, state) * entry[:, lanes]
            for pair in range(4):
                weights = []
                for h in (2 * pair, 2 * pair + 1):
                    col = HH * i + HG * g + h
                    gap = cum_ref[:, col : col + 1] - key_ref[col : col + 1, :]
                    weights.append((jnp.exp(jnp.where(keeps[i], gap, -jnp.inf)) * scores[4 * i + g]).astype(BF16))
                lanes = pl.ds(GW * g + T * pair, T)
                x = x_tile(x_ref, here, 4 * g + pair)
                zero = jnp.zeros_like(x)
                both = jnp.concatenate([jnp.where(left, x, zero), jnp.where(left, zero, x)], axis=0)
                out = dot(jnp.concatenate(weights, axis=1), both) + skip_ref[:, lanes] * x.astype(F32)
                if i == 1:
                    out += carried[:, T * pair : T * pair + T]
                out_ref[here, lanes] = out
    mine_ref[...] = out_ref[pl.ds(pl.multiple_of(T * core, T), T), :]
    other = out_ref[there, :]
    high = other.astype(BF16)
    swap_ref[:, pl.ds(0, HW)] = high
    swap_ref[:, pl.ds(HW, HW)] = (other - high.astype(F32)).astype(BF16)
    swap_ref[:, pl.ds(2 * HW, 2 * T)] = bc_ref[there, pl.ds(2 * T, 2 * T)]
    swap_ref[:, pl.ds(2 * HW + 2 * T, T)] = of_span(carry, 1 - core)
    tails = sums_ref[...]
    sums = tails + pltpu.roll(tails, T - HH, 1) + pltpu.roll(tails, T - 2 * HH, 1)
    rows = iota((8, T), 0)
    sums = jnp.where(rows == 6, tails, sums)
    sums = jnp.concatenate([sums, jnp.zeros((T - 8, T), F32)], axis=0).T[:NP]
    resets = sums[:, 6:7]
    sums = jnp.where(iota((NP, T), 1) < HP, sums[:, 4:5], sums[:, 5:6])
    decay_ref[...] = jnp.where(resets == 0.0, jnp.exp(-sums * pair_ref[...]), 0.0)


def scan_kernel(in_ref, decay_ref, out_ref):
    h = jnp.zeros((32, T), F32)
    for p in range(NP):
        at = (p % NX) * NZ + p // NX
        out_ref[at] = h.astype(BF16)
        h = decay_ref[pl.ds(p, 1), :] * h + in_ref[at].astype(F32)


def entering(h_ref, g):
    return jnp.concatenate(
        [jnp.concatenate([h_ref[8 * g + 2 * p], h_ref[8 * g + 2 * p + 1]], axis=0) for p in range(4)], axis=1
    )


def mine_kernel(partial_ref, bc_ref, factor_ref, h_ref, swap_ref, out_ref, scale_ref, partial2_ref, c2_ref):
    core = lax.axis_index("c")
    e = expander()
    scale = dot(factor_ref[...], e)
    cs = bc_ref[pl.ds(pl.multiple_of(T * core, T), T), pl.ds(2 * T, 2 * T)]
    for g in range(4):
        lanes = pl.ds(GW * g, GW)
        inter = dot(cs[:, N * g : N * g + N], entering(h_ref, g)) * scale[:, GW * g : GW * g + GW]
        out_ref[:, lanes] = (partial_ref[:, lanes] + inter).astype(BF16)
    c2_ref[...] = swap_ref[:, pl.ds(2 * HW, 2 * T)]
    scale_ref[...] = dot(swap_ref[:, pl.ds(2 * HW + 2 * T, T)], e)
    for g in range(4):
        lanes = pl.ds(GW * g, GW)
        low = swap_ref[:, pl.ds(HW + GW * g, GW)]
        partial2_ref[:, lanes] = swap_ref[:, lanes].astype(F32) + low.astype(F32)


def final_kernel(mine_ref, scale_ref, partial_ref, c_ref, h_ref, out_hbm, other_ref, sems):
    core = lax.axis_index("c")

    def copy(src, n, half):
        return pltpu.make_async_copy(src, out_hbm.at[:, pl.ds(HW * half, HW)], sems.at[n])

    for k in range(2):

        @pl.when(core == k)
        def _():
            copy(mine_ref, 0, k).start()

    cs = c_ref[...]
    for g in range(4):
        lanes = pl.ds(GW * g, GW)
        inter = dot(cs[:, N * g : N * g + N], entering(h_ref, g)) * scale_ref[:, lanes]
        partial = partial_ref[:, lanes]
        other_ref[:, lanes] = (partial + inter).astype(BF16)
    for k in range(2):

        @pl.when(core == k)
        def _():
            copy(other_ref, 1, 1 - k).start()
            copy(mine_ref, 0, k).wait()
            copy(other_ref, 1, 1 - k).wait()


def per_device(x, b, c, dt, order, resets, rate, skip):
    core = lax.axis_index("c")
    sds = jax.ShapeDtypeStruct
    hbm, vmem = pl.BlockSpec(memory_space=pltpu.HBM), pl.BlockSpec(memory_space=pltpu.VMEM)
    resets = resets.reshape(1, T)
    packed = pl.pallas_call(
        pack_kernel,
        out_shape=sds((NZ, 2 * NX, MSG, T), BF16),
        in_specs=[hbm] * 5,
        out_specs=hbm,
        scratch_shapes=[
            pltpu.VMEM(x.shape, BF16),
            pltpu.VMEM(b.shape, BF16),
            pltpu.VMEM(c.shape, BF16),
            pltpu.VMEM(dt.shape[::-1], BF16),
            pltpu.VMEM((1, T), I32),
            pltpu.VMEM((NZ, 2 * NX, MSG, T), BF16),
            pltpu.SemaphoreType.DMA((2 + 3 * len(PARTS),)),
            pltpu.SemaphoreType.DMA((len(PARTS),)),
        ],
        compiler_params=params(56),
        name="pack",
    )(x, b, c, dt.T, resets)
    packed = packed.reshape(2 * NP, MSG, T)
    arrived = lax.all_to_all(packed, ("z", "x", "c"), split_axis=0, concat_axis=0, tiled=True)
    order2 = lax.ppermute(order, "c", [(0, 1), (1, 0)])
    resets2 = lax.ppermute(resets, "c", [(0, 1), (1, 0)])
    perm, cnt = pl.pallas_call(
        plan_kernel,
        out_shape=(sds((2 * T, 2 * T), BF16), sds((T, T), F32)),
        compiler_params=params(16),
        cost_estimate=pl.CostEstimate(flops=1_000_000_000, bytes_accessed=1_000_000, transcendentals=0),
        name="plan",
    )(order, order2, resets, resets2)
    mine = lax.dynamic_slice_in_dim(rate, core * HH, HH)
    rate_row = jnp.concatenate([mine, mine, jnp.zeros((64,), F32)]).reshape(1, T)
    pair = (lax.axis_index("x") * NZ + lax.axis_index("z")) // 2 * 2
    pair_row = jnp.repeat(lax.dynamic_slice_in_dim(rate, core * HH + pair, 2), HP).reshape(1, T)
    skip_row = jnp.repeat(lax.dynamic_slice_in_dim(skip, core * HH, HH), HP).reshape(1, HW)
    xs, bc, cum, step, msg, sums = pl.pallas_call(
        state_kernel,
        out_shape=(
            sds((AWAY, HW), BF16),
            sds((2 * T, 4 * T), BF16),
            sds((T, T), F32),
            sds((T, T), F32),
            sds((NP, 32, T), BF16),
            sds((8, T), F32),
        ),
        out_specs=(hbm,) + (vmem,) * 3 + (hbm, vmem),
        scratch_shapes=[
            pltpu.VMEM((2 * T, HW), BF16),
            pltpu.SemaphoreType.DMA((4,)),
            pltpu.VMEM((NP, 32, T), BF16),
            pltpu.SemaphoreType.DMA((4,)),
        ],
        compiler_params=params(24),
        name="state",
    )(arrived, rate_row, perm, cnt)
    totals = lax.all_to_all(msg, ("x", "z"), split_axis=0, concat_axis=0, tiled=True)
    partial, factors, swap, decays = pl.pallas_call(
        local_kernel,
        out_shape=(sds((T, HW), F32), sds((T, T), BF16), sds((T, 2 * HW + 3 * T), BF16), sds((NP, T), F32)),
        in_specs=[hbm] + [vmem] * 7,
        scratch_shapes=[
            pltpu.VMEM((2 * T, HW), F32),
            pltpu.VMEM((T, T), F32),
            pltpu.VMEM((2 * T, HW), BF16),
            pltpu.SemaphoreType.DMA,
        ],
        compiler_params=params(20),
        cost_estimate=pl.CostEstimate(flops=2_000_000_000, bytes_accessed=6_000_000, transcendentals=1_100_000),
        name="local",
    )(xs, bc, cum, step, cnt, skip_row, sums, pair_row)
    swap = lax.ppermute(swap, "c", [(0, 1), (1, 0)])
    prefixes = pl.pallas_call(
        scan_kernel, out_shape=sds((NP, 32, T), BF16), compiler_params=params(16), name="chips"
    )(totals, decays)
    states = lax.all_to_all(prefixes, ("x", "z"), split_axis=0, concat_axis=0, tiled=True)
    other = lax.ppermute(states, "c", [(0, 1), (1, 0)])
    own, scale, partial2, c2 = pl.pallas_call(
        mine_kernel,
        out_shape=(sds((T, HW), BF16), sds((T, HW), F32), sds((T, HW), F32), sds((T, 2 * T), BF16)),
        compiler_params=params(20),
        name="mine",
    )(partial, bc, factors, states, swap)
    return pl.pallas_call(
        final_kernel,
        out_shape=sds((T, 2 * HW), BF16),
        in_specs=[vmem] * 5,
        out_specs=hbm,
        scratch_shapes=[pltpu.VMEM((T, HW), BF16), pltpu.SemaphoreType.DMA((2,))],
        compiler_params=params(20),
        name="final",
    )(own, scale, partial2, c2, other)


def solution(mesh):
    fine = Mesh(mesh.devices.reshape(NZ, NX, 2, mesh.shape["seq"]), ("z", "x", "c", "seq"))
    rows = ("seq", "z", "x", "c")
    in_specs = (P(rows, None),) * 5 + (P(rows), P(), P())
    return jax.shard_map(
        per_device, mesh=fine, in_specs=in_specs, out_specs=P(rows, None), check_vma=False
    )
```

```python
import jax
import jax.numpy as jnp
from jax import lax
from jax.experimental import pallas as pl
from jax.experimental.pallas import tpu as pltpu
from jax.sharding import Mesh, PartitionSpec as P

F32 = jnp.float32
BF16 = jnp.bfloat16
I32 = jnp.int32
T = 128
NX, NZ = 4, 8
NP = NX * NZ
HG = 8
HP = 64
N = 64
GW = HG * HP
HH = 32
HW = HH * HP
MSG = 88
PARTS = (48, 64, 16)
AWAY = 12288


def iota(shape, dim):
    return lax.broadcasted_iota(I32, shape, dim)


def dot(a, b):
    return jnp.dot(a, b, preferred_element_type=F32)


def dot_nt(a, b):
    return lax.dot_general(a, b, (((1,), (1,)), ((), ())), preferred_element_type=F32)


def params(mib):
    return pltpu.CompilerParams(vmem_limit_bytes=mib * 1024 * 1024)


def softplus(v):
    return jnp.maximum(v, 0.0) + jnp.log1p(jnp.exp(-jnp.abs(v)))


def three_parts(v):
    high = v.astype(BF16)
    rest = v - high.astype(F32)
    mid = rest.astype(BF16)
    return high, mid, (rest - mid.astype(F32)).astype(BF16)


def pack_kernel(
    x_hbm, b_hbm, c_hbm, dt_hbm, reset_hbm, out_hbm,
    x_ref, b_ref, c_ref, dt_ref, reset_ref, out_ref, sems, out_sems,
):
    pairs = [(reset_hbm, reset_ref), (dt_hbm, dt_ref)]
    for part, span in enumerate(PARTS):
        rows = pl.ds(sum(PARTS[:part]), span)
        pairs += [(src.at[rows], dst.at[rows]) for src, dst in ((b_hbm, b_ref), (c_hbm, c_ref), (x_hbm, x_ref))]
    copies = [pltpu.make_async_copy(s, d, sems.at[n]) for n, (s, d) in enumerate(pairs)]
    for copy in copies:
        copy.start()
    picks = []
    for span in PARTS:
        row, col = iota((4 * span, 4 * span), 0), iota((4 * span, 4 * span), 1)
        pick = (col // span == (row % 16) // 4) & (col % span == (row // 16) * 4 + row % 4)
        picks.append(pick.astype(BF16))
    lane, head = iota((256, 64), 0), iota((256, 64), 1)
    spread = (lane % T < HH) & (head == (lane // T) * HH + lane % T)
    to, row = iota((256, T), 0), iota((256, T), 1)
    own_row = ((to % 8 < 4) & (row == (to // 8) * 4 + to % 8)).astype(BF16)
    to, head = iota((256, 64), 0), iota((256, 64), 1)
    chosen = ((to % 8 // 2 == 2) & (head == 2 * (to // 8) + to % 2)).astype(BF16)
    of_chip = (iota((T, T), 0) // 4 == iota((T, T), 1)).astype(BF16)
    chip = lax.axis_index("z") * NX + lax.axis_index("x")
    flag = (iota((8, T), 0) == 6) & (iota((8, T), 1) == chip)
    for copy in copies[:2]:
        copy.wait()
    dt = dt_ref[...]
    wide = dot(spread.astype(BF16), dt).astype(BF16)
    steps = dot_nt(own_row, wide)
    sums = dot(jnp.concatenate(three_parts(softplus(dt.astype(F32))), axis=0), of_chip)
    high, mid, low = three_parts(sums[:64] + sums[64:128] + sums[128:])
    sums = high.astype(F32) + pltpu.roll(mid.astype(F32), HH, 1) + pltpu.roll(low.astype(F32), 2 * HH, 1)
    sums = dot(chosen, sums.astype(BF16))
    resets = jnp.sum(reset_ref[...].astype(F32), axis=1, keepdims=True)
    flag = jnp.where(flag, jnp.broadcast_to(resets, (8, T)), 0.0)
    sent = []
    for part, span in enumerate(PARTS):
        for copy in copies[2 + 3 * part : 5 + 3 * part]:
            copy.wait()
        start = sum(PARTS[:part])
        rows = pl.ds(start, span)
        tiles = []
        for c in range(2):
            for q in range(4):
                tiles.append([x_ref[rows, pl.ds(HW * c + 512 * q + T * j, T)] for j in range(4)])
            tiles.append(
                [b_ref[rows, pl.ds(256 * c, T)], b_ref[rows, pl.ds(256 * c + T, T)],
                 c_ref[rows, pl.ds(256 * c, T)], c_ref[rows, pl.ds(256 * c + T, T)]]
            )
        right = jnp.concatenate([jnp.concatenate(t, axis=0) for t in tiles], axis=1)
        got = dot(picks[part], right).astype(BF16)
        for p in range(span // 4):
            z, x = start // 16 + p // NX, p % NX
            at = 8 * (start // 4 + p)
            for c in range(2):
                to = 2 * x + c
                for q in range(5):
                    lanes = slice(T * (5 * c + q), T * (5 * c + q) + T)
                    out_ref[z, to, pl.ds(16 * q, 16), :] = got[16 * p : 16 * p + 16, lanes]
                m = 8 * (16 * c + (NZ * x + z) // 2)
                tail = steps[at : at + 8, T * c : T * c + T] + sums[m : m + 8] + flag
                out_ref[z, to, pl.ds(80, 8), :] = tail.astype(BF16)
        here = pl.ds(start // 16, span // 16)
        sent.append(pltpu.make_async_copy(out_ref.at[here], out_hbm.at[here], out_sems.at[part]))
        sent[-1].start()
    for copy in sent:
        copy.wait()


def columns(row):
    return jnp.broadcast_to(row, (T, T)).T


def plan_kernel(order_ref, order2_ref, reset_ref, reset2_ref, perm_ref, cnt_ref):
    core = lax.axis_index("c")
    orders = [order_ref[...].astype(F32), order2_ref[...].astype(F32)]
    resets = [reset_ref[...].astype(F32), reset2_ref[...].astype(F32)]
    orders = [columns(jnp.where(core == i, orders[0], orders[1])) for i in range(2)]
    upto = (iota((T, T), 0) <= iota((T, T), 1)).astype(BF16)
    counts = []
    for i in range(2):
        row = jnp.broadcast_to(jnp.where(core == i, resets[0], resets[1]), (8, T))
        counts.append(columns(dot(row.astype(BF16), upto)[:1]))
    cnt_ref[...] = jnp.where(iota((T, T), 1) < HH, counts[0], counts[1])
    order = jnp.concatenate(orders, axis=0).astype(I32)
    source = order >> 1
    target = (source << 2) + ((iota((256, T), 0) >> 7) << 1) + (order & 1)
    for m in range(2):
        perm_ref[:, pl.ds(T * m, T)] = jnp.where(iota((256, T), 1) + T * m == target, 1.0, 0.0).astype(BF16)


def expander():
    gap = iota((T, T), 0) % HH - iota((T, T), 1) // HP
    return jnp.concatenate([jnp.where(gap == 2 * t, 1.0, 0.0).astype(BF16) for t in range(HW // T)], axis=1)


def two_parts(v):
    high = v.astype(BF16).astype(F32)
    low = v - high
    return jnp.where(iota(v.shape, 1) < 64, high, pltpu.roll(low, 64, 1))


def of_span(parts, i):
    return jnp.where((iota(parts.shape, 1) % 64) // HH == i, parts, 0.0).astype(BF16)


def inner_weights(cum, step, cnt):
    last, last_cnt = cum[T - 1 : T], cnt[T - 1 : T]
    return two_parts(jnp.where(cnt == last_cnt, jnp.exp(last - cum) * step, 0.0))


def span_decay(cum, cnt):
    return jnp.where(cnt[T - 1 : T] == 0.0, jnp.exp(cum[T - 1 : T]), 0.0)


def x_tile(x_ref, rows, t):
    return x_ref[rows, pl.ds(T * (4 * (t % 4) + t // 4), T)]


def state_kernel(
    arrived_ref, rate_ref, perm_ref, cnt_ref, x_hbm, bc_ref, cum_ref, step_ref, msg_hbm, sums_ref, x_ref, x_sems, msg_ref, msg_sems
):
    top = iota((NP, 8, T), 1) < 4

    def halves(here):
        even, odd = here[:, 0], here[:, 1]
        low = jnp.where(top, even, pltpu.roll(odd, 4, 1)).reshape(256, T).astype(BF16)
        high = jnp.where(top, pltpu.roll(even, 4, 1), odd).reshape(256, T).astype(BF16)
        return low, high

    perm = perm_ref[...]
    cnt = cnt_ref[...]
    tails = arrived_ref[:, pl.ds(80, 8), :].astype(F32)
    sums_ref[...] = jnp.sum(tails, axis=0)
    raw = dot(perm, halves(tails.reshape(NP, 2, 8, T))[0])
    raw = jnp.where(iota((T, T), 1) < HH, raw[:T], pltpu.roll(raw[T:], HH, 1))
    step = softplus(raw)
    lower = (iota((T, T), 0) >= iota((T, T), 1)).astype(BF16)
    cum = dot(lower, jnp.concatenate(three_parts(-step * rate_ref[...]), axis=1))
    cum = cum[:, :T] + cum[:, T : 2 * T] + cum[:, 2 * T :]
    cum_ref[...] = cum
    step_ref[...] = step
    tiles = [[] for _ in range(4)]
    for q in range(5):
        here = arrived_ref[:, pl.ds(16 * q, 16), :].astype(F32).reshape(NP, 2, 2, 8, T)
        for half in range(2):
            low, high = halves(here[:, :, half])
            tiles[2 * half].append(low)
            tiles[2 * half + 1].append(high)
    x_copies = []
    for j in range(4):
        rows = dot(perm, jnp.concatenate(tiles[j], axis=1)).astype(BF16)
        here = pl.ds(GW * j, GW)
        x_ref[:, here] = rows[:, :GW]
        bc_ref[:, pl.ds(T * j, T)] = rows[:, GW:]
        x_copies.append(pltpu.make_async_copy(x_ref.at[:, here], x_hbm.at[pl.ds(0, 2 * T), here], x_sems.at[j]))
        x_copies[-1].start()
    e = expander()
    coef = inner_weights(cum, step, cnt)
    decay = two_parts(jnp.broadcast_to(span_decay(cum, cnt), (8, T)))
    decay = dot(of_span(decay, 1), e)[:1]
    weighted = []
    for i in range(2):
        here = pl.ds(T * i, T)
        scale = dot(of_span(coef, i), e)
        weighted.append([(x_tile(x_ref, here, t).astype(F32) * scale[:, T * t : T * t + T]).astype(BF16) for t in range(16)])
    for tile in range(2):
        b = [bc_ref[pl.ds(T * i, T), pl.ds(T * tile, T)].astype(F32).T.astype(BF16) for i in range(2)]
        for half in range(2):
            g = 2 * tile + half
            lanes = slice(GW * g, GW * g + GW)
            states = [dot(b[i][N * half : N * half + N], jnp.concatenate(weighted[i][4 * g : 4 * g + 4], axis=1)) for i in range(2)]
            h = (decay[:, lanes] * states[0] + states[1]).astype(BF16)
            for pair in range(4):
                for k in range(2):
                    m = (4 * g + pair) * 2 + k
                    msg_ref[m] = h[32 * k : 32 * k + 32, T * pair : T * pair + T]
            part = pl.ds(8 * g, 8)
            x_copies.append(pltpu.make_async_copy(msg_ref.at[part], msg_hbm.at[part], msg_sems.at[g]))
            x_copies[-1].start()
    for copy in x_copies:
        copy.wait()


def local_kernel(
    x_hbm, bc_ref, cum_ref, step_ref, cnt_ref, skip_ref, sums_ref, pair_ref,
    mine_ref, factor_ref, swap_ref, decay_ref, out_ref, key_ref, x_ref, x_sem,
):
    x_copy = pltpu.make_async_copy(x_hbm.at[pl.ds(0, 2 * T)], x_ref, x_sem)
    x_copy.start()
    core = lax.axis_index("c")
    there = pl.ds(pl.multiple_of(T * (1 - core), T), T)
    cum, step, cnt = cum_ref[...], step_ref[...], cnt_ref[...]
    key_ref[...] = (cum - jnp.log(step)).T
    entry = jnp.where(cnt == 0.0, jnp.exp(cum), 0.0)
    decay = jnp.broadcast_to(span_decay(cum, cnt), (8, T))
    before = jnp.where(iota((8, T), 1) < HH, 1.0, pltpu.roll(decay, HH, 1))
    carry = two_parts(entry * before[:1])
    factor_ref[...] = of_span(carry, core)
    e = expander()
    entry = dot(of_span(two_parts(entry), 1), e)
    causal = iota((T, T), 0) >= iota((T, T), 1)
    keeps, scores = [], []
    for i in range(2):
        here = pl.ds(T * i, T)
        count = jnp.broadcast_to(cnt[:, HH * i : HH * i + 1], (T, T))
        keeps.append(causal & (count == count.T))
        for g in range(4):
            lanes = slice(N * (g % 2), N * (g % 2) + N)
            b = bc_ref[here, pl.ds(T * (g // 2), T)][:, lanes]
            c = bc_ref[here, pl.ds(2 * T + T * (g // 2), T)][:, lanes]
            scores.append(dot_nt(c, b))
    x_copy.wait()
    inner = dot(of_span(inner_weights(cum, step, cnt), 0), e)
    weighted = [
        (x_tile(x_ref, pl.ds(0, T), t).astype(F32) * inner[:, T * t : T * t + T]).astype(BF16) for t in range(16)
    ]
    left = iota((T, T), 1) < HP
    for i in range(2):
        here = pl.ds(T * i, T)
        for g in range(4):
            tile, half = g // 2, g % 2
            if i == 1:
                c = bc_ref[here, pl.ds(2 * T + T * tile, T)][:, N * half : N * half + N]
                lanes = slice(GW * g, GW * g + GW)
                first = bc_ref[pl.ds(0, T), pl.ds(T * tile, T)].astype(F32).T[N * half : N * half + N].astype(BF16)
                state = dot(first, jnp.concatenate(weighted[4 * g : 4 * g + 4], axis=1)).astype(BF16)
                carried = dot(c, state) * entry[:, lanes]
            for pair in range(4):
                weights = []
                for h in (2 * pair, 2 * pair + 1):
                    col = HH * i + HG * g + h
                    gap = cum_ref[:, col : col + 1] - key_ref[col : col + 1, :]
                    weights.append((jnp.exp(jnp.where(keeps[i], gap, -jnp.inf)) * scores[4 * i + g]).astype(BF16))
                lanes = pl.ds(GW * g + T * pair, T)
                x = x_tile(x_ref, here, 4 * g + pair)
                zero = jnp.zeros_like(x)
                both = jnp.concatenate([jnp.where(left, x, zero), jnp.where(left, zero, x)], axis=0)
                out = dot(jnp.concatenate(weights, axis=1), both) + skip_ref[:, lanes] * x.astype(F32)
                if i == 1:
                    out += carried[:, T * pair : T * pair + T]
                out_ref[here, lanes] = out
    mine_ref[...] = out_ref[pl.ds(pl.multiple_of(T * core, T), T), :]
    other = out_ref[there, :]
    high = other.astype(BF16)
    swap_ref[:, pl.ds(0, HW)] = high
    swap_ref[:, pl.ds(HW, HW)] = (other - high.astype(F32)).astype(BF16)
    swap_ref[:, pl.ds(2 * HW, 2 * T)] = bc_ref[there, pl.ds(2 * T, 2 * T)]
    swap_ref[:, pl.ds(2 * HW + 2 * T, T)] = of_span(carry, 1 - core)
    tails = sums_ref[...]
    sums = tails + pltpu.roll(tails, T - HH, 1) + pltpu.roll(tails, T - 2 * HH, 1)
    rows = iota((8, T), 0)
    sums = jnp.where(rows == 6, tails, sums)
    sums = jnp.concatenate([sums, jnp.zeros((T - 8, T), F32)], axis=0).T[:NP]
    resets = sums[:, 6:7]
    sums = jnp.where(iota((NP, T), 1) < HP, sums[:, 4:5], sums[:, 5:6])
    decay_ref[...] = jnp.where(resets == 0.0, jnp.exp(-sums * pair_ref[...]), 0.0)


def scan_kernel(in_ref, decay_ref, out_ref):
    h = jnp.zeros((32, T), F32)
    for p in range(NP):
        at = (p % NX) * NZ + p // NX
        out_ref[at] = h.astype(BF16)
        h = decay_ref[pl.ds(p, 1), :] * h + in_ref[at].astype(F32)


def entering(h_ref, g):
    return jnp.concatenate(
        [jnp.concatenate([h_ref[8 * g + 2 * p], h_ref[8 * g + 2 * p + 1]], axis=0) for p in range(4)], axis=1
    )


def mine_kernel(partial_ref, bc_ref, factor_ref, h_ref, swap_ref, out_ref, scale_ref, partial2_ref, c2_ref):
    core = lax.axis_index("c")
    e = expander()
    scale = dot(factor_ref[...], e)
    cs = bc_ref[pl.ds(pl.multiple_of(T * core, T), T), pl.ds(2 * T, 2 * T)]
    for g in range(4):
        lanes = pl.ds(GW * g, GW)
        inter = dot(cs[:, N * g : N * g + N], entering(h_ref, g)) * scale[:, GW * g : GW * g + GW]
        out_ref[:, lanes] = (partial_ref[:, lanes] + inter).astype(BF16)
    c2_ref[...] = swap_ref[:, pl.ds(2 * HW, 2 * T)]
    scale_ref[...] = dot(swap_ref[:, pl.ds(2 * HW + 2 * T, T)], e)
    for g in range(4):
        lanes = pl.ds(GW * g, GW)
        low = swap_ref[:, pl.ds(HW + GW * g, GW)]
        partial2_ref[:, lanes] = swap_ref[:, lanes].astype(F32) + low.astype(F32)


def final_kernel(mine_ref, scale_ref, partial_ref, c_ref, h_ref, out_hbm, other_ref, sems):
    core = lax.axis_index("c")

    def copy(src, n, half):
        return pltpu.make_async_copy(src, out_hbm.at[:, pl.ds(HW * half, HW)], sems.at[n])

    for k in range(2):

        @pl.when(core == k)
        def _():
            copy(mine_ref, 0, k).start()

    cs = c_ref[...]
    for g in range(4):
        lanes = pl.ds(GW * g, GW)
        inter = dot(cs[:, N * g : N * g + N], entering(h_ref, g)) * scale_ref[:, lanes]
        partial = partial_ref[:, lanes]
        other_ref[:, lanes] = (partial + inter).astype(BF16)
    for k in range(2):

        @pl.when(core == k)
        def _():
            copy(other_ref, 1, 1 - k).start()
            copy(mine_ref, 0, k).wait()
            copy(other_ref, 1, 1 - k).wait()


def per_device(x, b, c, dt, order, resets, rate, skip):
    core = lax.axis_index("c")
    sds = jax.ShapeDtypeStruct
    hbm, vmem = pl.BlockSpec(memory_space=pltpu.HBM), pl.BlockSpec(memory_space=pltpu.VMEM)
    resets = resets.reshape(1, T)
    packed = pl.pallas_call(
        pack_kernel,
        out_shape=sds((NZ, 2 * NX, MSG, T), BF16),
        in_specs=[hbm] * 5,
        out_specs=hbm,
        scratch_shapes=[
            pltpu.VMEM(x.shape, BF16),
            pltpu.VMEM(b.shape, BF16),
            pltpu.VMEM(c.shape, BF16),
            pltpu.VMEM(dt.shape[::-1], BF16),
            pltpu.VMEM((1, T), I32),
            pltpu.VMEM((NZ, 2 * NX, MSG, T), BF16),
            pltpu.SemaphoreType.DMA((2 + 3 * len(PARTS),)),
            pltpu.SemaphoreType.DMA((len(PARTS),)),
        ],
        compiler_params=params(56),
        name="pack",
    )(x, b, c, dt.T, resets)
    packed = packed.reshape(2 * NP, MSG, T)
    arrived = lax.all_to_all(packed, ("z", "x", "c"), split_axis=0, concat_axis=0, tiled=True)
    order2 = lax.ppermute(order, "c", [(0, 1), (1, 0)])
    resets2 = lax.ppermute(resets, "c", [(0, 1), (1, 0)])
    perm, cnt = pl.pallas_call(
        plan_kernel,
        out_shape=(sds((2 * T, 2 * T), BF16), sds((T, T), F32)),
        compiler_params=params(16),
        cost_estimate=pl.CostEstimate(flops=1_000_000_000, bytes_accessed=1_000_000, transcendentals=0),
        name="plan",
    )(order, order2, resets, resets2)
    mine = lax.dynamic_slice_in_dim(rate, core * HH, HH)
    rate_row = jnp.concatenate([mine, mine, jnp.zeros((64,), F32)]).reshape(1, T)
    pair = (lax.axis_index("x") * NZ + lax.axis_index("z")) // 2 * 2
    pair_row = jnp.repeat(lax.dynamic_slice_in_dim(rate, core * HH + pair, 2), HP).reshape(1, T)
    skip_row = jnp.repeat(lax.dynamic_slice_in_dim(skip, core * HH, HH), HP).reshape(1, HW)
    xs, bc, cum, step, msg, sums = pl.pallas_call(
        state_kernel,
        out_shape=(
            sds((AWAY, HW), BF16),
            sds((2 * T, 4 * T), BF16),
            sds((T, T), F32),
            sds((T, T), F32),
            sds((NP, 32, T), BF16),
            sds((8, T), F32),
        ),
        out_specs=(hbm,) + (vmem,) * 3 + (hbm, vmem),
        scratch_shapes=[
            pltpu.VMEM((2 * T, HW), BF16),
            pltpu.SemaphoreType.DMA((4,)),
            pltpu.VMEM((NP, 32, T), BF16),
            pltpu.SemaphoreType.DMA((4,)),
        ],
        compiler_params=params(24),
        name="state",
    )(arrived, rate_row, perm, cnt)
    totals = lax.all_to_all(msg, ("x", "z"), split_axis=0, concat_axis=0, tiled=True)
    partial, factors, swap, decays = pl.pallas_call(
        local_kernel,
        out_shape=(sds((T, HW), F32), sds((T, T), BF16), sds((T, 2 * HW + 3 * T), BF16), sds((NP, T), F32)),
        in_specs=[hbm] + [vmem] * 7,
        scratch_shapes=[
            pltpu.VMEM((2 * T, HW), F32),
            pltpu.VMEM((T, T), F32),
            pltpu.VMEM((2 * T, HW), BF16),
            pltpu.SemaphoreType.DMA,
        ],
        compiler_params=params(20),
        cost_estimate=pl.CostEstimate(flops=2_000_000_000, bytes_accessed=6_000_000, transcendentals=1_100_000),
        name="local",
    )(xs, bc, cum, step, cnt, skip_row, sums, pair_row)
    swap = lax.ppermute(swap, "c", [(0, 1), (1, 0)])
    prefixes = pl.pallas_call(
        scan_kernel, out_shape=sds((NP, 32, T), BF16), compiler_params=params(16), name="chips"
    )(totals, decays)
    states = lax.all_to_all(prefixes, ("x", "z"), split_axis=0, concat_axis=0, tiled=True)
    other = lax.ppermute(states, "c", [(0, 1), (1, 0)])
    own, scale, partial2, c2 = pl.pallas_call(
        mine_kernel,
        out_shape=(sds((T, HW), BF16), sds((T, HW), F32), sds((T, HW), F32), sds((T, 2 * T), BF16)),
        compiler_params=params(20),
        name="mine",
    )(partial, bc, factors, states, swap)
    return pl.pallas_call(
        final_kernel,
        out_shape=sds((T, 2 * HW), BF16),
        in_specs=[vmem] * 5,
        out_specs=hbm,
        scratch_shapes=[pltpu.VMEM((T, HW), BF16), pltpu.SemaphoreType.DMA((2,))],
        compiler_params=params(20),
        name="final",
    )(own, scale, partial2, c2, other)


def solution(mesh):
    fine = Mesh(mesh.devices.reshape(NZ, NX, 2, mesh.shape["seq"]), ("z", "x", "c", "seq"))
    rows = ("seq", "z", "x", "c")
    in_specs = (P(rows, None),) * 5 + (P(rows), P(), P())
    return jax.shard_map(
        per_device, mesh=fine, in_specs=in_specs, out_specs=P(rows, None), check_vma=False
    )
```
